512 devices in a mesh: row: 8 (over z_hi, core), col: 8 (over x, z_lo), dep: 8 (over y).
Axes of the slice: x: 4, y: 8, z: 8 (z_hi: 4, z_lo: 2; z = z_hi * 2 + z_lo), core: 2. Of those that a mesh axis runs over, the one named last changes fastest.
Arguments:
- tokens: bfloat16 [1024, 8192], P('row', ('dep', 'col')), may hold values from -30 to 30
- w_gate: bfloat16 [8192, 16384], P('dep', ('col', 'row')), may hold values from -0.0625 to 0.0625
- w_up: bfloat16 [8192, 16384], P('dep', ('col', 'row')), may hold values from -0.0625 to 0.0625
- upstream: bfloat16 [1024, 16384], P('row', ('col', 'dep')), may hold values from -6 to 6
- history: float32 [16, 3], replicated, may hold values from 2 to 24
Outputs:
- hidden: bfloat16 [1024, 16384], P('row', ('col', 'dep'))
- input_grad: bfloat16 [1024, 8192], P('row', ('dep', 'col'))
- gate_grad: bfloat16 [8192, 16384], P('dep', ('col', 'row'))
- upper_grad: bfloat16 [8192, 16384], P('dep', ('col', 'row'))
- new_history: float32 [16, 3], replicated
The draws below stay inside these ranges and needn't reach their ends.
All inputs are finite; a program needn't handle non-finite values.
Results may differ from the reference program's by a relative error of at most 0.0085.
Values may be sent and summed in bfloat16 or wider, within the bound.
No kernel may reach another device: no remote copies, remote signals or barrier semaphores. Data moves between devices by JAX's collectives and lax.ppermute only.
A program may use at most 64 MiB of HBM per device.

```python
import jax
import jax.numpy as jnp

D = 8192
FF = 16384
HIST = 16
TOKENS = 1024


def draw_tokens(key, part):
    key = jax.random.fold_in(key, 11)
    base_key, column_key = jax.random.split(key)
    base = jnp.clip(jax.random.normal(base_key, (TOKENS, D), jnp.float32), -5.0, 5.0)
    rising = 1.0 + 2.0 * jnp.arange(TOKENS, dtype=jnp.float32)[:, None] / TOKENS
    column_scale = jnp.exp(jnp.log(2.0) * jax.random.uniform(column_key, (1, D), jnp.float32))
    return (base * rising * column_scale).astype(jnp.bfloat16)


def draw_history(key, part):
    key = jax.random.fold_in(key, 23)
    lower = jnp.array([8.0, 2.0, 4.0], jnp.float32)
    upper = jnp.array([24.0, 12.0, 12.0], jnp.float32)
    spread = jax.random.uniform(key, (HIST, 3), jnp.float32)
    return lower + (upper - lower) * spread


def block_scale(key, dims, cuts, smallest, high):
    def one(dim, parts):
        steps = jax.random.uniform(jax.random.fold_in(jax.random.fold_in(key, 6), dim), (parts,), jnp.float32, smallest / len(cuts), high / len(cuts))
        return jnp.repeat(jnp.exp(steps), dims[dim] // parts).reshape((-1,) + (1,) * (len(dims) - dim - 1))

    factor_of = one(*cuts[0])
    for cut in cuts[1:]:
        factor_of = factor_of * one(*cut)
    return factor_of


def bell_draw(rng, shape, scale, most, cuts=(), kind=jnp.bfloat16):
    level = block_scale(rng, shape, cuts, -0.22, 0.18) if cuts else 1.0
    drawn = jax.random.normal(rng, shape, jnp.float32) * scale * level
    return jnp.minimum(jnp.maximum(drawn, -most), most).astype(kind)


def setup_inputs(seed: int = 0) -> dict:
    keys = jax.random.split(jax.random.key(seed), 6)
    return {
        "tokens": draw_tokens(jax.random.fold_in(keys[5], 71), 0),
        "w_gate": bell_draw(keys[1], (D, FF), D ** -0.5, 0.0625, ((0, 8), (1, 64))),
        "w_up": bell_draw(keys[2], (D, FF), D ** -0.5, 0.0625, ((0, 8), (1, 64))),
        "upstream": bell_draw(keys[3], (TOKENS, FF), 1.0, 6.0, ((0, 8), (1, 64))),
        "history": draw_history(jax.random.fold_in(keys[5], 71), 0),
    }


def reference(tokens, w_gate, w_up, upstream, history):
    tops = jnp.max(history, axis=0)
    scale_in = 448.0 / tops[0]
    scale_grad = 448.0 / tops[2]
    tok_float = tokens.astype(jnp.float32)
    quant_in = jnp.clip(tok_float * scale_in, -448.0, 448.0).astype(jnp.bfloat16)
    gate_sum = jnp.dot(quant_in, w_gate, preferred_element_type=jnp.float32) / scale_in
    lift_sum = jnp.dot(quant_in, w_up, preferred_element_type=jnp.float32) / scale_in
    sigmoid_gate = jax.nn.sigmoid(gate_sum)
    activated = gate_sum * sigmoid_gate
    hidden = (activated * lift_sum).astype(jnp.bfloat16)
    grad_in = upstream.astype(jnp.float32)
    grad_gate = grad_in * lift_sum * sigmoid_gate * (1.0 + gate_sum * (1.0 - sigmoid_gate))
    grad_lift = grad_in * activated
    quant_gate = jnp.clip(grad_gate * scale_grad, -448.0, 448.0).astype(jnp.bfloat16)
    quant_lift = jnp.clip(grad_lift * scale_grad, -448.0, 448.0).astype(jnp.bfloat16)
    back_sum = jnp.dot(quant_gate, w_gate.T, preferred_element_type=jnp.float32) + jnp.dot(quant_lift, w_up.T, preferred_element_type=jnp.float32)
    input_grad = (back_sum / scale_grad).astype(jnp.bfloat16)
    divisor = scale_in * scale_grad * TOKENS
    gate_grad = (jnp.dot(quant_in.T, quant_gate, preferred_element_type=jnp.float32) / divisor).astype(jnp.bfloat16)
    upper_grad = (jnp.dot(quant_in.T, quant_lift, preferred_element_type=jnp.float32) / divisor).astype(jnp.bfloat16)
    peak_in = jnp.max(jnp.abs(tok_float))
    peak_hidden = jnp.max(jnp.abs(hidden.astype(jnp.float32)))
    peak_grad = jnp.maximum(jnp.max(jnp.abs(grad_gate)), jnp.max(jnp.abs(grad_lift)))
    peaks = jnp.stack([peak_in, peak_hidden, peak_grad])
    new_history = jnp.concatenate([history[1:], peaks[None, :]], axis=0)
    return hidden, input_grad, gate_grad, upper_grad, new_history
```

```python
import jax
import jax.numpy as jnp
from jax import lax
from jax.experimental import pallas as pl
from jax.experimental.pallas import tpu as pltpu
from jax.sharding import Mesh
from jax.sharding import PartitionSpec as P

F32 = jnp.float32
BF16 = jnp.bfloat16
VMEM = pl.BlockSpec(memory_space=pltpu.VMEM)
SMEM = pl.BlockSpec(memory_space=pltpu.SMEM)


def params():
    return pltpu.CompilerParams(vmem_limit_bytes=40 * 1024 * 1024)


def call(body, outs, args, flops=0, moved=0, scratch=()):
    return pl.pallas_call(
        body,
        out_shape=[jax.ShapeDtypeStruct(s, t) for s, t in outs],
        in_specs=[SMEM if a.dtype == jnp.int32 else VMEM for a in args],
        out_specs=[VMEM] * len(outs),
        scratch_shapes=list(scratch),
        compiler_params=params(),
        cost_estimate=pl.CostEstimate(flops=flops, bytes_accessed=moved, transcendentals=0),
    )(*args)


def top(values):
    return jnp.max(jnp.max(values, axis=0, keepdims=True), axis=1, keepdims=True)


def rows_of(*values):
    row = lax.broadcasted_iota(jnp.int32, (8, 128), 0)
    tile = jnp.zeros((8, 128), F32)
    for i, v in enumerate(values):
        tile = jnp.where(row == i, v, tile)
    return tile


def pack_peaks(peak_in, peak_hidden, peak_grad):
    high = peak_grad.astype(BF16).astype(F32)
    rest = peak_grad - high
    mid = rest.astype(BF16).astype(F32)
    return rows_of(peak_in, peak_hidden, high, mid, rest - mid).astype(BF16)


def unpack_peaks(packed):
    grads = packed[:, 2, :] + packed[:, 3, :] + packed[:, 4, :]
    return top(packed[:, 0, :]), top(packed[:, 1, :]), top(grads)


def scale_body(hist_ref, tok_ref, out_ref, scal_ref):
    tops = jnp.max(hist_ref[...], axis=0, keepdims=True)
    scale_in = 448.0 / tops[:, 0:1]
    scale_grad = 448.0 / tops[:, 2:3]
    tok = tok_ref[...].astype(F32)
    quant = jnp.clip(tok * scale_in, -448.0, 448.0).astype(BF16)
    for i in range(out_ref.shape[0]):
        out_ref[i] = quant
    scal_ref[...] = rows_of(scale_in, scale_grad, top(jnp.abs(tok)))


def forward_body(core_ref, x_ref, g0_ref, u0_ref, g1_ref, u1_ref, out_ref, xh_ref):
    groups, cols, rows = out_ref.shape[0] // 2, x_ref.shape[0] // (out_ref.shape[0] // 2), x_ref.shape[1]
    core = core_ref[0]
    for g in range(groups):
        for k in range(cols):
            xh_ref[g * rows : (g + 1) * rows, k * 128 : (k + 1) * 128] = x_ref[g * cols + k]
    x = xh_ref[...]
    for which, pair in enumerate(((g0_ref, u0_ref), (g1_ref, u1_ref))):
        place = core if which == 0 else 1 - core
        for half, w_ref in enumerate(pair):
            part = jnp.dot(x, w_ref[...], preferred_element_type=F32).astype(BF16)
            for g in range(groups):
                out_ref[2 * g + place, half * rows : (half + 1) * rows, :] = part[g * rows : (g + 1) * rows]


def middle_body(in_ref, up_ref, scal_ref, hidden_ref, q_ref):
    rows = up_ref.shape[0]
    scale_in = scal_ref[0:1, 0:1]
    scale_grad = scal_ref[1:2, 0:1]
    gate_sum = jnp.sum(in_ref[:, :rows, :].astype(F32), axis=0) / scale_in
    lift_sum = jnp.sum(in_ref[:, rows:, :].astype(F32), axis=0) / scale_in
    sigmoid_gate = 1.0 / (1.0 + jnp.exp(-gate_sum))
    activated = gate_sum * sigmoid_gate
    hidden = (activated * lift_sum).astype(BF16)
    hidden_ref[...] = hidden
    grad_in = up_ref[...].astype(F32)
    grad_gate = grad_in * lift_sum * sigmoid_gate * (1.0 + gate_sum * (1.0 - sigmoid_gate))
    grad_lift = grad_in * activated
    quant_gate = jnp.clip(grad_gate * scale_grad, -448.0, 448.0).astype(BF16)
    quant_lift = jnp.clip(grad_lift * scale_grad, -448.0, 448.0).astype(BF16)
    peak_grad = jnp.maximum(top(jnp.abs(grad_gate)), top(jnp.abs(grad_lift)))
    peaks = pack_peaks(scal_ref[2:3, 0:1], top(jnp.abs(hidden.astype(F32))), peak_grad)
    wide = jnp.concatenate([peaks, peaks], axis=1)
    wide = jnp.concatenate([wide, wide], axis=0)
    for i in range(q_ref.shape[0]):
        q_ref[i, :rows, :] = quant_gate
        q_ref[i, rows : 2 * rows, :] = quant_lift
        q_ref[i, 2 * rows :, :] = wide


def backward_body(core_ref, q_ref, g0_ref, u0_ref, g1_ref, u1_ref, out_ref, mine_ref, send_ref):
    groups = q_ref.shape[0] // 2
    rows = (q_ref.shape[1] - 16) // 2
    cols = out_ref.shape[0] // groups
    core = core_ref[0]
    contract = (((1,), (1,)), ((), ()))
    total = None
    for which, pair in enumerate(((g0_ref, u0_ref), (g1_ref, u1_ref))):
        place = core if which == 0 else 1 - core
        kept = mine_ref if which == 0 else send_ref
        for half, w_ref in enumerate(pair):
            for g in range(groups):
                kept[half, g * rows : (g + 1) * rows, :] = q_ref[2 * g + place, half * rows : (half + 1) * rows, :]
            part = lax.dot_general(kept[half], w_ref[...], contract, preferred_element_type=F32)
            total = part if total is None else total + part
    packed = pack_peaks(*unpack_peaks(q_ref[:, 2 * rows : 2 * rows + 16, 0:128].astype(F32)[:, 0:8, :]))
    for g in range(groups):
        for k in range(cols):
            out_ref[g * cols + k, :rows, :] = total[g * rows : (g + 1) * rows, k * 128 : (k + 1) * 128].astype(BF16)
            out_ref[g * cols + k, rows:, :] = packed


def last_body(in_ref, scal_ref, out_ref, peaks_ref):
    rows = out_ref.shape[0]
    out_ref[...] = (jnp.sum(in_ref[:, :rows, :].astype(F32), axis=0) / scal_ref[1:2, 0:1]).astype(BF16)
    peaks_ref[...] = rows_of(*unpack_peaks(in_ref[:, rows:, :].astype(F32)))


def history_body(hist_ref, mine_ref, other_ref, out_ref):
    peaks = jnp.maximum(mine_ref[...], other_ref[...])
    col = lax.broadcasted_iota(jnp.int32, (1, 3), 1)
    row = jnp.where(col == 0, peaks[0:1, 0:1], jnp.where(col == 1, peaks[1:2, 0:1], peaks[2:3, 0:1]))
    past = hist_ref.shape[0] - 1
    out_ref[0:past, :] = hist_ref[1:, :]
    out_ref[past:, :] = row


def per_device(sizes, tokens, w_gate, w_up, upstream, history):
    nh, nx, nw, ny = (sizes[a] for a in "hxwy")
    plane = ("h", "x", "w")
    count = nh * nx * nw
    rows, width = tokens.shape
    depth, units = w_gate.shape
    swap = [(0, 1), (1, 0)]
    turn = [(h * ny + y, (y // 2) * ny + h * 2 + y % 2) for h in range(nh) for y in range(ny)]
    core = lax.axis_index("c").reshape(1)

    copies, scal = call(scale_body, [((count, rows, width), BF16), ((8, 128), F32)], (history, tokens))
    up = lax.ppermute(upstream, ("h", "y"), turn)
    gate_other = lax.ppermute(w_gate, "c", swap)
    lift_other = lax.ppermute(w_up, "c", swap)
    weights = (w_gate, w_up, gate_other, lift_other)
    x_all = lax.all_to_all(copies, plane, 0, 0, tiled=True)

    work = 8 * nh * rows * depth * units
    parts, x_mine = call(
        forward_body,
        [((ny, 2 * rows, units), BF16), ((nh * rows, depth), BF16)],
        (core, x_all) + weights,
        flops=work,
        moved=6 * 2**20,
    )
    sums = lax.all_to_all(parts, "y", 0, 0, tiled=True)
    x_other = lax.ppermute(x_mine, "c", swap)
    hidden, quants = call(
        middle_body, [((rows, units), BF16), ((ny, 2 * rows + 16, units), BF16)], (sums, up, scal), moved=2**21
    )
    q_all = lax.all_to_all(quants, "y", 0, 0, tiled=True)
    hidden = lax.ppermute(hidden, ("h", "y"), turn)
    back, q_mine, q_send = call(
        backward_body,
        [((count, rows + 8, width), BF16), ((2, nh * rows, units), BF16), ((2, nh * rows, units), BF16)],
        (core, q_all) + weights,
        flops=work,
        moved=6 * 2**20,
    )
    back_all = lax.all_to_all(back, plane, 0, 0, tiled=True)
    q_other = lax.ppermute(q_send, "c", swap)
    divisor = scal[0, 0] * scal[1, 0] * (2 * nh * rows)
    contract = (((0,), (0,)), ((), ()))
    grads = []
    for i in range(2):
        total = lax.dot_general(x_mine, q_mine[i], contract, preferred_element_type=F32) + lax.dot_general(
            x_other, q_other[i], contract, preferred_element_type=F32
        )
        grads.append((total / divisor).astype(BF16))
    input_grad, peaks = call(last_body, [((rows, width), BF16), ((8, 128), F32)], (back_all, scal), moved=2**21)
    peaks_other = lax.ppermute(peaks, "c", swap)
    (new_history,) = call(history_body, [(history.shape, F32)], (history, peaks, peaks_other))
    return (hidden, input_grad, grads[0], grads[1], new_history)


def solution(mesh):
    sizes = dict(h=mesh.shape["row"] // 2, c=2, x=mesh.shape["col"] // 2, w=2, y=mesh.shape["dep"])
    fine = Mesh(mesh.devices.reshape(tuple(sizes.values())), tuple(sizes))
    row, col = ("h", "c"), ("x", "w")
    placed = (
        P(row, ("y",) + col),
        P("y", col + row),
        P("y", col + row),
        P(row, col + ("y",)),
        P(),
    )

    def step(*args):
        return per_device(sizes, *args)

    return jax.shard_map(
        step,
        mesh=fine,
        in_specs=placed,
        out_specs=(P(row, col + ("y",)), P(row, ("y",) + col), P("y", col + row), P("y", col + row), P()),
        check_vma=False,
    )
```

```python
import jax
import jax.numpy as jnp
from jax import lax
from jax.experimental import pallas as pl
from jax.experimental.pallas import tpu as pltpu
from jax.sharding import Mesh
from jax.sharding import PartitionSpec as P

F32 = jnp.float32
BF16 = jnp.bfloat16
VMEM = pl.BlockSpec(memory_space=pltpu.VMEM)
HBM = pl.BlockSpec(memory_space=pltpu.HBM)
SMEM = pl.BlockSpec(memory_space=pltpu.SMEM)


def params():
    return pltpu.CompilerParams(vmem_limit_bytes=16 * 1024 * 1024)


def call(body, outs, args, flops=0, moved=0, scratch=(), far=(), far_outs=()):
    return pl.pallas_call(
        body,
        out_shape=[jax.ShapeDtypeStruct(s, t) for s, t in outs],
        in_specs=[SMEM if a.dtype == jnp.int32 else HBM if i in far else VMEM for i, a in enumerate(args)],
        out_specs=[HBM if i in far_outs else VMEM for i in range(len(outs))],
        scratch_shapes=list(scratch),
        compiler_params=params(),
        cost_estimate=pl.CostEstimate(flops=flops, bytes_accessed=moved, transcendentals=0),
    )(*args)


def fetched(sources, held_ref, sems):
    copies = [pltpu.make_async_copy(ref, held_ref.at[i], sems.at[i]) for i, ref in enumerate(sources)]
    for copy in copies:
        copy.start()
    return copies


def top(values):
    return jnp.max(jnp.max(values, axis=0, keepdims=True), axis=1, keepdims=True)


def rows_of(*values):
    row = lax.broadcasted_iota(jnp.int32, (8, 128), 0)
    tile = jnp.zeros((8, 128), F32)
    for i, v in enumerate(values):
        tile = jnp.where(row == i, v, tile)
    return tile


def scale_body(hist_ref, tok_ref, out_ref, scal_ref):
    tops = jnp.max(hist_ref[...], axis=0, keepdims=True)
    scale_in = 448.0 / tops[:, 0:1]
    scale_grad = 448.0 / tops[:, 2:3]
    tok = tok_ref[...].astype(F32)
    quant = jnp.clip(tok * scale_in, -448.0, 448.0).astype(BF16)
    for i in range(out_ref.shape[0]):
        out_ref[i] = quant
    scal_ref[...] = rows_of(scale_in, scale_grad, top(jnp.abs(tok)))


def forward_body(place_ref, x_ref, g0_ref, u0_ref, g1_ref, u1_ref, out_ref, xh_ref, held_ref, sems):
    groups, cols, rows = out_ref.shape[0] // 2, x_ref.shape[0] // (out_ref.shape[0] // 2), x_ref.shape[1]
    copies = fetched((g0_ref, u0_ref, g1_ref, u1_ref), held_ref, sems)
    core, turned = place_ref[0], place_ref[1]
    for g in range(groups):
        for k in range(cols):
            xh_ref[g * rows : (g + 1) * rows, k * 128 : (k + 1) * 128] = x_ref[g * cols + k]
    x = xh_ref[...]
    for i, copy in enumerate(copies):
        place, half = (core if i < 2 else 1 - core), i % 2
        copy.wait()
        part = jnp.dot(x, held_ref[i], preferred_element_type=F32).astype(BF16)
        for g in range(groups):
            piece = 2 * lax.rem(turned + g, groups) + place
            out_ref[piece, half * rows : (half + 1) * rows, :] = part[g * rows : (g + 1) * rows]


def middle_body(in_ref, up_ref, scal_ref, hidden_ref, q_ref, peaks_ref):
    rows = up_ref.shape[0]
    scale_in = scal_ref[0:1, 0:1]
    scale_grad = scal_ref[1:2, 0:1]
    gate_sum = jnp.sum(in_ref[:, :rows, :].astype(F32), axis=0) / scale_in
    lift_sum = jnp.sum(in_ref[:, rows:, :].astype(F32), axis=0) / scale_in
    sigmoid_gate = 1.0 / (1.0 + jnp.exp(-gate_sum))
    activated = gate_sum * sigmoid_gate
    hidden = (activated * lift_sum).astype(BF16)
    hidden_ref[...] = hidden
    grad_in = up_ref[...].astype(F32)
    grad_gate = grad_in * lift_sum * sigmoid_gate * (1.0 + gate_sum * (1.0 - sigmoid_gate))
    grad_lift = grad_in * activated
    quant_gate = jnp.clip(grad_gate * scale_grad, -448.0, 448.0).astype(BF16)
    quant_lift = jnp.clip(grad_lift * scale_grad, -448.0, 448.0).astype(BF16)
    peak_grad = jnp.maximum(top(jnp.abs(grad_gate)), top(jnp.abs(grad_lift)))
    peaks_ref[...] = rows_of(scal_ref[2:3, 0:1], top(jnp.abs(hidden.astype(F32))), peak_grad)
    for i in range(q_ref.shape[0]):
        q_ref[i, :rows, :] = quant_gate
        q_ref[i, rows:, :] = quant_lift


def backward_body(
    place_ref, q_ref, g0_ref, u0_ref, g1_ref, u1_ref, out_ref, mine_ref, send_ref, held_ref, sems, kept_ref, out_sems
):
    groups = q_ref.shape[0] // 2
    rows = q_ref.shape[1] // 2
    cols = out_ref.shape[0] // groups
    copies = fetched((g0_ref, u0_ref, g1_ref, u1_ref), held_ref, sems)
    core, turned = place_ref[0], place_ref[1]
    contract = (((1,), (1,)), ((), ()))
    for i in range(4):
        which, half = i // 2, i % 2
        place = core if which == 0 else 1 - core
        for g in range(groups):
            piece = 2 * lax.rem(turned + g, groups) + place
            kept_ref[which, half, g * rows : (g + 1) * rows, :] = q_ref[piece, half * rows : (half + 1) * rows, :]
    sends = [
        pltpu.make_async_copy(kept_ref.at[which], far_ref, out_sems.at[which])
        for which, far_ref in ((1, send_ref), (0, mine_ref))
    ]
    for send in sends:
        send.start()
    total = None
    for i, copy in enumerate(copies):
        copy.wait()
        part = lax.dot_general(kept_ref[i // 2, i % 2], held_ref[i], contract, preferred_element_type=F32)
        total = part if total is None else total + part
    for g in range(groups):
        for k in range(cols):
            out_ref[g * cols + k] = total[g * rows : (g + 1) * rows, k * 128 : (k + 1) * 128].astype(BF16)
    for send in sends:
        send.wait()


def last_body(in_ref, scal_ref, hist_ref, peaks_ref, hidden_ref, out_ref, next_ref, hidden_out_ref):
    out_ref[...] = (jnp.sum(in_ref[...].astype(F32), axis=0) / scal_ref[1:2, 0:1]).astype(BF16)
    col = lax.broadcasted_iota(jnp.int32, (1, 3), 1)
    peaks = [peaks_ref[i : i + 1, 0:1] for i in range(3)]
    past = hist_ref.shape[0] - 1
    next_ref[0:past, :] = hist_ref[1:, :]
    next_ref[past:, :] = jnp.where(col == 0, peaks[0], jnp.where(col == 1, peaks[1], peaks[2]))
    hidden_out_ref[...] = hidden_ref[...]


def flips(n):
    bits = [1 << b for b in range(n.bit_length() - 1)]
    return [[(i, i ^ b) for i in range(n)] for b in bits]


def merged(peaks, axis, n):
    for perm in flips(n):
        peaks = jnp.maximum(peaks, lax.ppermute(peaks, axis, perm))
    return peaks


def per_device(sizes, tokens, w_gate, w_up, upstream, history):
    nh, nx, nw, ny = (sizes[a] for a in "hxwy")
    plane = ("h", "x", "w")
    count = nh * nx * nw
    rows, width = tokens.shape
    depth, units = w_gate.shape
    swap = [(0, 1), (1, 0)]
    spots = [(h, a, b) for h in range(nh) for a in range(nh) for b in range(2)]
    at = lambda h, a, b: h * ny + 2 * (a % nh) + b
    along_y = [(at(h, a, b), at(h, a + h, b)) for h, a, b in spots]
    along_z = [(at(h, a, b), at((a - h) % nh, a, b)) for h, a, b in spots]
    back_y = [(j, i) for i, j in along_y]
    place = jnp.stack([lax.axis_index("c"), lax.axis_index("h")])

    copies, scal = call(scale_body, [((count, rows, width), BF16), ((8, 128), F32)], (history, tokens))
    x_all = lax.all_to_all(copies, plane, 0, 0, tiled=True)
    gate_other = lax.ppermute(w_gate, "c", swap)
    lift_other = lax.ppermute(w_up, "c", swap)
    up = lax.ppermute(upstream, ("h", "y"), along_y)
    x_all, gate_other, lift_other, up = lax.optimization_barrier((x_all, gate_other, lift_other, up))
    weights = (w_gate, w_up, gate_other, lift_other)

    held = [pltpu.VMEM((4, depth, units), BF16), pltpu.SemaphoreType.DMA((4,))]
    work = 8 * nh * rows * depth * units
    parts, x_mine = call(
        forward_body,
        [((ny, 2 * rows, units), BF16), ((nh * rows, depth), BF16)],
        (place, x_all) + weights,
        flops=work,
        moved=6 * 2**20,
        scratch=held,
        far=range(2, 6),
    )
    parts, x_mine, up = lax.optimization_barrier((parts, x_mine, up))
    sums = lax.all_to_all(parts, "y", 0, 0, tiled=True)
    up = lax.ppermute(up, ("h", "y"), along_z)
    x_other = lax.ppermute(x_mine, "c", swap)
    sums, up, x_other = lax.optimization_barrier((sums, up, x_other))
    hidden, quants, peaks = call(
        middle_body,
        [((rows, units), BF16), ((ny, 2 * rows, units), BF16), ((8, 128), F32)],
        (sums, up, scal),
        moved=2**21,
    )
    q_all = lax.all_to_all(quants, "y", 0, 0, tiled=True)
    hidden = lax.ppermute(hidden, ("h", "y"), along_z)
    peaks = merged(merged(merged(peaks, "c", 2), "x", nx), ("h", "w"), nh * nw)
    q_all, hidden, peaks = lax.optimization_barrier((q_all, hidden, peaks))
    back, q_mine, q_send = call(
        backward_body,
        [((count, rows, width), BF16), ((2, nh * rows, units), BF16), ((2, nh * rows, units), BF16)],
        (place, q_all) + weights,
        flops=work,
        moved=6 * 2**20,
        scratch=held + [pltpu.VMEM((2, 2, nh * rows, units), BF16), pltpu.SemaphoreType.DMA((2,))],
        far=range(2, 6),
        far_outs=(1, 2),
    )
    back, q_send, hidden, peaks = lax.optimization_barrier((back, q_send, hidden, peaks))
    back_all = lax.all_to_all(back, plane, 0, 0, tiled=True)
    q_other = lax.ppermute(q_send, "c", swap)
    hidden = lax.ppermute(hidden, ("h", "y"), back_y)
    peaks = merged(peaks, "y", ny)
    divisor = scal[0, 0] * scal[1, 0] * (2 * nh * rows)
    contract = (((0,), (0,)), ((), ()))
    grads = []
    for i in range(2):
        total = lax.dot_general(x_mine, q_mine[i], contract, preferred_element_type=F32) + lax.dot_general(
            x_other, q_other[i], contract, preferred_element_type=F32
        )
        grads.append((total / divisor).astype(BF16))
    back_all, grads = lax.optimization_barrier((back_all, grads))
    input_grad, new_history, hidden = call(
        last_body,
        [((rows, width), BF16), (history.shape, F32), ((rows, units), BF16)],
        (back_all, scal, history, peaks, hidden),
        moved=2**21,
    )
    return (hidden, input_grad, grads[0], grads[1], new_history)


def solution(mesh):
    sizes = dict(h=mesh.shape["row"] // 2, c=2, x=mesh.shape["col"] // 2, w=2, y=mesh.shape["dep"])
    fine = Mesh(mesh.devices.reshape(tuple(sizes.values())), tuple(sizes))
    row, col = ("h", "c"), ("x", "w")
    placed = (
        P(row, ("y",) + col),
        P("y", col + row),
        P("y", col + row),
        P(row, col + ("y",)),
        P(),
    )

    def step(*args):
        return per_device(sizes, *args)

    return jax.shard_map(
        step,
        mesh=fine,
        in_specs=placed,
        out_specs=(P(row, col + ("y",)), P(row, ("y",) + col), P("y", col + row), P("y", col + row), P()),
        check_vma=False,
    )
```

```python
import jax
import jax.numpy as jnp
from jax import lax
from jax.experimental import pallas as pl
from jax.experimental.pallas import tpu as pltpu
from jax.sharding import Mesh
from jax.sharding import PartitionSpec as P

F32 = jnp.float32
BF16 = jnp.bfloat16
VMEM = pl.BlockSpec(memory_space=pltpu.VMEM)
SMEM = pl.BlockSpec(memory_space=pltpu.SMEM)


def params():
    return pltpu.CompilerParams(vmem_limit_bytes=16 * 1024 * 1024)


def call(body, outs, args, flops=0, moved=0, scratch=()):
    return pl.pallas_call(
        body,
        out_shape=[jax.ShapeDtypeStruct(s, t) for s, t in outs],
        in_specs=[SMEM if a.dtype == jnp.int32 else VMEM for a in args],
        out_specs=[VMEM] * len(outs),
        scratch_shapes=list(scratch),
        compiler_params=params(),
        cost_estimate=pl.CostEstimate(flops=flops, bytes_accessed=moved, transcendentals=0),
    )(*args)


def top(values):
    return jnp.max(jnp.max(values, axis=0, keepdims=True), axis=1, keepdims=True)


def rows_of(*values):
    row = lax.broadcasted_iota(jnp.int32, (8, 128), 0)
    tile = jnp.zeros((8, 128), F32)
    for i, v in enumerate(values):
        tile = jnp.where(row == i, v, tile)
    return tile


def pack_peaks(peak_in, peak_hidden, peak_grad):
    high = peak_grad.astype(BF16).astype(F32)
    rest = peak_grad - high
    mid = rest.astype(BF16).astype(F32)
    return rows_of(peak_in, peak_hidden, high, mid, rest - mid).astype(BF16)


def unpack_peaks(packed):
    grads = packed[:, 2, :] + packed[:, 3, :] + packed[:, 4, :]
    return top(packed[:, 0, :]), top(packed[:, 1, :]), top(grads)


def scale_body(hist_ref, tok_ref, out_ref, scal_ref):
    tops = jnp.max(hist_ref[...], axis=0, keepdims=True)
    scale_in = 448.0 / tops[:, 0:1]
    scale_grad = 448.0 / tops[:, 2:3]
    tok = tok_ref[...].astype(F32)
    quant = jnp.clip(tok * scale_in, -448.0, 448.0).astype(BF16)
    for i in range(out_ref.shape[0]):
        out_ref[i] = quant
    scal_ref[...] = rows_of(scale_in, scale_grad, top(jnp.abs(tok)))


def forward_body(place_ref, x_ref, g0_ref, u0_ref, g1_ref, u1_ref, out_ref, xh_ref):
    groups, cols, rows = out_ref.shape[0] // 2, x_ref.shape[0] // (out_ref.shape[0] // 2), x_ref.shape[1]
    core, turned = place_ref[0], place_ref[1]
    for g in range(groups):
        spot = pl.ds(pl.multiple_of(lax.rem(turned + g, groups) * rows, rows), rows)
        for k in range(cols):
            xh_ref[spot, k * 128 : (k + 1) * 128] = x_ref[g * cols + k]
    x = xh_ref[...]
    for which, pair in enumerate(((g0_ref, u0_ref), (g1_ref, u1_ref))):
        place = core if which == 0 else 1 - core
        for half, w_ref in enumerate(pair):
            part = jnp.dot(x, w_ref[...], preferred_element_type=F32).astype(BF16)
            for g in range(groups):
                out_ref[2 * g + place, half * rows : (half + 1) * rows, :] = part[g * rows : (g + 1) * rows]


def middle_body(in_ref, up_ref, scal_ref, hidden_ref, q_ref):
    rows = up_ref.shape[0]
    scale_in = scal_ref[0:1, 0:1]
    scale_grad = scal_ref[1:2, 0:1]
    gate_sum = jnp.sum(in_ref[:, :rows, :].astype(F32), axis=0) / scale_in
    lift_sum = jnp.sum(in_ref[:, rows:, :].astype(F32), axis=0) / scale_in
    sigmoid_gate = 1.0 / (1.0 + jnp.exp(-gate_sum))
    activated = gate_sum * sigmoid_gate
    hidden = (activated * lift_sum).astype(BF16)
    hidden_ref[...] = hidden
    grad_in = up_ref[...].astype(F32)
    grad_gate = grad_in * lift_sum * sigmoid_gate * (1.0 + gate_sum * (1.0 - sigmoid_gate))
    grad_lift = grad_in * activated
    quant_gate = jnp.clip(grad_gate * scale_grad, -448.0, 448.0).astype(BF16)
    quant_lift = jnp.clip(grad_lift * scale_grad, -448.0, 448.0).astype(BF16)
    peak_grad = jnp.maximum(top(jnp.abs(grad_gate)), top(jnp.abs(grad_lift)))
    peaks = pack_peaks(scal_ref[2:3, 0:1], top(jnp.abs(hidden.astype(F32))), peak_grad)
    wide = jnp.concatenate([peaks, peaks], axis=1)
    for i in range(q_ref.shape[0]):
        q_ref[i, :rows, :] = quant_gate
        q_ref[i, rows : 2 * rows, :] = quant_lift
        q_ref[i, 2 * rows :, :] = wide


def backward_body(place_ref, q_ref, g0_ref, u0_ref, g1_ref, u1_ref, out_ref, kept_ref):
    groups = q_ref.shape[0] // 2
    rows = (q_ref.shape[1] - 8) // 2
    cols = out_ref.shape[0] // groups
    core, turned = place_ref[0], place_ref[1]
    contract = (((1,), (1,)), ((), ()))
    total = None
    for which, pair in enumerate(((g0_ref, u0_ref), (g1_ref, u1_ref))):
        place = core if which == 0 else 1 - core
        for half, w_ref in enumerate(pair):
            for g in range(groups):
                kept_ref[g * rows : (g + 1) * rows, :] = q_ref[2 * g + place, half * rows : (half + 1) * rows, :]
            part = lax.dot_general(kept_ref[...], w_ref[...], contract, preferred_element_type=F32)
            total = part if total is None else total + part
    packed = pack_peaks(*unpack_peaks(q_ref[:, 2 * rows :, 0:128].astype(F32)))
    for g in range(groups):
        first = lax.rem(groups + g - turned, groups) * cols
        for k in range(cols):
            out_ref[first + k, :rows, :] = total[g * rows : (g + 1) * rows, k * 128 : (k + 1) * 128].astype(BF16)
            out_ref[first + k, rows:, :] = packed


def last_body(in_ref, scal_ref, hidden_ref, out_ref, peaks_ref, hidden_out_ref):
    rows = out_ref.shape[0]
    out_ref[...] = (jnp.sum(in_ref[:, :rows, :].astype(F32), axis=0) / scal_ref[1:2, 0:1]).astype(BF16)
    peaks_ref[...] = rows_of(*unpack_peaks(in_ref[:, rows:, :].astype(F32)))
    hidden_out_ref[...] = hidden_ref[...]


def history_body(hist_ref, mine_ref, other_ref, out_ref):
    peaks = jnp.maximum(mine_ref[...], other_ref[...])
    col = lax.broadcasted_iota(jnp.int32, (1, 3), 1)
    row = jnp.where(col == 0, peaks[0:1, 0:1], jnp.where(col == 1, peaks[1:2, 0:1], peaks[2:3, 0:1]))
    past = hist_ref.shape[0] - 1
    out_ref[0:past, :] = hist_ref[1:, :]
    out_ref[past:, :] = row


def per_device(sizes, tokens, w_gate, w_up, upstream, history):
    nh, nx, nw, ny = (sizes[a] for a in "hxwy")
    plane = ("h", "x", "w")
    count = nh * nx * nw
    rows, width = tokens.shape
    depth, units = w_gate.shape
    swap = [(0, 1), (1, 0)]
    spots = [(h, a, b) for h in range(nh) for a in range(nh) for b in range(2)]
    at = lambda h, a, b: h * ny + 2 * (a % nh) + b
    along_y = [(at(h, a, b), at(h, a + h, b)) for h, a, b in spots]
    along_z = [(at(h, a, b), at((a - h) % nh, a, b)) for h, a, b in spots]
    back_y = [(j, i) for i, j in along_y]
    core = lax.axis_index("c")
    place = jnp.stack([core, lax.axis_index("h")])

    copies, scal = call(scale_body, [((count, rows, width), BF16), ((8, 128), F32)], (history, tokens))
    x_all = lax.all_to_all(copies, plane, 0, 0, tiled=True)
    gate_other = lax.ppermute(w_gate, "c", swap)
    lift_other = lax.ppermute(w_up, "c", swap)
    up = lax.ppermute(upstream, ("h", "y"), along_y)
    x_all, gate_other, lift_other, up = lax.optimization_barrier((x_all, gate_other, lift_other, up))

    work = 8 * nh * rows * depth * units
    parts, x_mine = call(
        forward_body,
        [((ny, 2 * rows, units), BF16), ((nh * rows, depth), BF16)],
        (place, x_all, w_gate, w_up, gate_other, lift_other),
        flops=work,
        moved=6 * 2**20,
    )
    parts, x_mine, up = lax.optimization_barrier((parts, x_mine, up))
    sums = lax.all_to_all(parts, "y", 0, 0, tiled=True)
    up = lax.ppermute(up, ("h", "y"), along_z)
    sums, up = lax.optimization_barrier((sums, up))
    hidden, quants = call(
        middle_body, [((rows, units), BF16), ((ny, 2 * rows + 8, units), BF16)], (sums, up, scal), moved=2**21
    )
    quants, x_mine = lax.optimization_barrier((quants, x_mine))
    q_all = lax.all_to_all(quants, "y", 0, 0, tiled=True)
    hidden = lax.ppermute(hidden, ("h", "y"), along_z)
    x_other = lax.ppermute(x_mine, "c", swap)
    q_all, hidden, x_other = lax.optimization_barrier((q_all, hidden, x_other))
    (back,) = call(
        backward_body,
        [((count, rows + 8, width), BF16)],
        (place, q_all, w_gate, w_up, gate_other, lift_other),
        flops=work,
        moved=6 * 2**20,
        scratch=[pltpu.VMEM((nh * rows, units), BF16)],
    )
    back, q_all, hidden = lax.optimization_barrier((back, q_all, hidden))
    back_all = lax.all_to_all(back, plane, 0, 0, tiled=True)
    hidden = lax.ppermute(hidden, ("h", "y"), back_y)
    q_parts = q_all[:, : 2 * rows].reshape(nh, 2, 2, rows, units)

    def chosen(which):
        part = lax.dynamic_index_in_dim(q_parts, which, 1, keepdims=False)
        return part.transpose(1, 0, 2, 3).reshape(2, nh * rows, units)

    q_other = lax.ppermute(chosen(1 - core), "c", swap)
    q_mine = chosen(core)
    divisor = scal[0, 0] * scal[1, 0] * (2 * nh * rows)
    contract = (((0,), (0,)), ((), ()))
    grads = []
    for i in range(2):
        total = lax.dot_general(x_mine, q_mine[i], contract, preferred_element_type=F32) + lax.dot_general(
            x_other, q_other[i], contract, preferred_element_type=F32
        )
        grads.append((total / divisor).astype(BF16))
    back_all, grads, hidden = lax.optimization_barrier((back_all, grads, hidden))
    input_grad, peaks, hidden = call(
        last_body,
        [((rows, width), BF16), ((8, 128), F32), ((rows, units), BF16)],
        (back_all, scal, hidden),
        moved=2**21,
    )
    peaks_other = lax.ppermute(peaks, "c", swap)
    (new_history,) = call(history_body, [(history.shape, F32)], (history, peaks, peaks_other))
    return (hidden, input_grad, grads[0], grads[1], new_history)


def solution(mesh):
    sizes = dict(h=mesh.shape["row"] // 2, c=2, x=mesh.shape["col"] // 2, w=2, y=mesh.shape["dep"])
    fine = Mesh(mesh.devices.reshape(tuple(sizes.values())), tuple(sizes))
    row, col = ("h", "c"), ("x", "w")
    placed = (
        P(row, ("y",) + col),
        P("y", col + row),
        P("y", col + row),
        P(row, col + ("y",)),
        P(),
    )

    def step(*args):
        return per_device(sizes, *args)

    return jax.shard_map(
        step,
        mesh=fine,
        in_specs=placed,
        out_specs=(P(row, col + ("y",)), P(row, ("y",) + col), P("y", col + row), P("y", col + row), P()),
        check_vma=False,
    )
```

```python
import jax
import jax.numpy as jnp
from jax import lax
from jax.experimental import pallas as pl
from jax.experimental.pallas import tpu as pltpu
from jax.sharding import Mesh
from jax.sharding import PartitionSpec as P

F32 = jnp.float32
BF16 = jnp.bfloat16
VMEM = pl.BlockSpec(memory_space=pltpu.VMEM)
SMEM = pl.BlockSpec(memory_space=pltpu.SMEM)


def params():
    return pltpu.CompilerParams(vmem_limit_bytes=16 * 1024 * 1024)


def call(body, outs, args, flops=0, moved=0, scratch=()):
    return pl.pallas_call(
        body,
        out_shape=[jax.ShapeDtypeStruct(s, t) for s, t in outs],
        in_specs=[SMEM if a.dtype == jnp.int32 else VMEM for a in args],
        out_specs=[VMEM] * len(outs),
        scratch_shapes=list(scratch),
        compiler_params=params(),
        cost_estimate=pl.CostEstimate(flops=flops, bytes_accessed=moved, transcendentals=0),
    )(*args)


def top(values):
    return jnp.max(jnp.max(values, axis=0, keepdims=True), axis=1, keepdims=True)


def rows_of(*values):
    row = lax.broadcasted_iota(jnp.int32, (8, 128), 0)
    tile = jnp.zeros((8, 128), F32)
    for i, v in enumerate(values):
        tile = jnp.where(row == i, v, tile)
    return tile


def pack_peaks(peak_in, peak_hidden, peak_grad):
    high = peak_grad.astype(BF16).astype(F32)
    rest = peak_grad - high
    mid = rest.astype(BF16).astype(F32)
    return rows_of(peak_in, peak_hidden, high, mid, rest - mid).astype(BF16)


def unpack_peaks(packed):
    grads = packed[:, 2, :] + packed[:, 3, :] + packed[:, 4, :]
    return top(packed[:, 0, :]), top(packed[:, 1, :]), top(grads)


def scale_body(hist_ref, tok_ref, out_ref, scal_ref):
    tops = jnp.max(hist_ref[...], axis=0, keepdims=True)
    scale_in = 448.0 / tops[:, 0:1]
    scale_grad = 448.0 / tops[:, 2:3]
    tok = tok_ref[...].astype(F32)
    quant = jnp.clip(tok * scale_in, -448.0, 448.0).astype(BF16)
    for i in range(out_ref.shape[0]):
        out_ref[i] = quant
    scal_ref[...] = rows_of(scale_in, scale_grad, top(jnp.abs(tok)))


def forward_body(place_ref, x_ref, g0_ref, u0_ref, g1_ref, u1_ref, out_ref, xh_ref):
    groups, cols, rows = out_ref.shape[0] // 2, x_ref.shape[0] // (out_ref.shape[0] // 2), x_ref.shape[1]
    core, turned = place_ref[0], place_ref[1]
    for g in range(groups):
        spot = pl.ds(pl.multiple_of(lax.rem(turned + g, groups) * rows, rows), rows)
        for k in range(cols):
            xh_ref[spot, k * 128 : (k + 1) * 128] = x_ref[g * cols + k]
    x = xh_ref[...]
    for which, pair in enumerate(((g0_ref, u0_ref), (g1_ref, u1_ref))):
        place = core if which == 0 else 1 - core
        for half, w_ref in enumerate(pair):
            part = jnp.dot(x, w_ref[...], preferred_element_type=F32).astype(BF16)
            for g in range(groups):
                out_ref[2 * g + place, half * rows : (half + 1) * rows, :] = part[g * rows : (g + 1) * rows]


def middle_body(in_ref, up_ref, scal_ref, hidden_ref, q_ref):
    rows = up_ref.shape[0]
    scale_in = scal_ref[0:1, 0:1]
    scale_grad = scal_ref[1:2, 0:1]
    gate_sum = jnp.sum(in_ref[:, :rows, :].astype(F32), axis=0) / scale_in
    lift_sum = jnp.sum(in_ref[:, rows:, :].astype(F32), axis=0) / scale_in
    sigmoid_gate = 1.0 / (1.0 + jnp.exp(-gate_sum))
    activated = gate_sum * sigmoid_gate
    hidden = (activated * lift_sum).astype(BF16)
    hidden_ref[...] = hidden
    grad_in = up_ref[...].astype(F32)
    grad_gate = grad_in * lift_sum * sigmoid_gate * (1.0 + gate_sum * (1.0 - sigmoid_gate))
    grad_lift = grad_in * activated
    quant_gate = jnp.clip(grad_gate * scale_grad, -448.0, 448.0).astype(BF16)
    quant_lift = jnp.clip(grad_lift * scale_grad, -448.0, 448.0).astype(BF16)
    peak_grad = jnp.maximum(top(jnp.abs(grad_gate)), top(jnp.abs(grad_lift)))
    peaks = pack_peaks(scal_ref[2:3, 0:1], top(jnp.abs(hidden.astype(F32))), peak_grad)
    wide = jnp.concatenate([peaks, peaks], axis=1)
    q_ref[:rows, :] = quant_gate
    q_ref[rows : 2 * rows, :] = quant_lift
    q_ref[2 * rows :, :] = wide


def gather(place_ref, piece_refs, kept_ref):
    count = len(piece_refs)
    rows = (piece_refs[0].shape[0] - 8) // 2
    for offset, ref in zip(ring_offsets(count), piece_refs):
        piece = lax.rem(place_ref[2] + (count + offset), count)
        which = lax.rem(piece + place_ref[0], 2)
        spot = pl.ds(pl.multiple_of(lax.div(piece, 2) * rows, rows), rows)
        for half in range(2):
            kept_ref[which, half, spot, :] = ref[half * rows : (half + 1) * rows, :]


def backward_body(place_ref, *refs):
    g0_ref, u0_ref, g1_ref, u1_ref, out_ref, kept_ref = refs[-6:]
    pieces = refs[:-6]
    rows = (pieces[0].shape[0] - 8) // 2
    groups = len(pieces) // 2
    cols = out_ref.shape[0]
    turned = place_ref[1]
    fine = (out_ref.shape[1] - 8) // (groups * rows)
    contract = (((1,), (1,)), ((), ()))
    gather(place_ref, pieces, kept_ref)
    total = None
    for i, w_ref in enumerate((g0_ref, u0_ref, g1_ref, u1_ref)):
        part = lax.dot_general(kept_ref[i // 2, i % 2], w_ref[...], contract, preferred_element_type=F32)
        total = part if total is None else total + part
    found = [unpack_peaks(ref[2 * rows :, 0:128].astype(F32)[None]) for ref in pieces]
    peaks = found[0]
    for other in found[1:]:
        peaks = [jnp.maximum(a, b) for a, b in zip(peaks, other)]
    packed = pack_peaks(*peaks)
    for k in range(cols):
        for g in range(groups):
            first = lax.rem(groups + g - turned, groups) * (fine * rows)
            for j in range(fine):
                lane = (k * fine + j) * 128
                spot = pl.ds(pl.multiple_of(first + j * rows, rows), rows)
                out_ref[k, spot, :] = total[g * rows : (g + 1) * rows, lane : lane + 128].astype(BF16)
        out_ref[k, groups * fine * rows :, :] = packed


def pick_body(place_ref, *refs):
    mine_ref, send_ref, kept_ref = refs[-3:]
    gather(place_ref, refs[:-3], kept_ref)
    mine_ref[...] = kept_ref[0]
    send_ref[...] = kept_ref[1]


def column_body(in_ref, out_ref):
    blocks, rows = out_ref.shape[0], out_ref.shape[1] - 8
    packed = pack_peaks(*unpack_peaks(in_ref[:, blocks * rows :, :].astype(F32)))
    for i in range(blocks):
        part = jnp.sum(in_ref[:, i * rows : (i + 1) * rows, :].astype(F32), axis=0)
        out_ref[i, :rows, :] = part.astype(BF16)
        out_ref[i, rows:, :] = packed


def last_body(in_ref, scal_ref, hidden_ref, out_ref, peaks_ref, hidden_out_ref):
    rows = out_ref.shape[0]
    out_ref[...] = (jnp.sum(in_ref[:, :rows, :].astype(F32), axis=0) / scal_ref[1:2, 0:1]).astype(BF16)
    peaks_ref[...] = rows_of(*unpack_peaks(in_ref[:, rows:, :].astype(F32)))
    hidden_out_ref[...] = hidden_ref[...]


def history_body(hist_ref, mine_ref, other_ref, out_ref):
    peaks = jnp.maximum(mine_ref[...], other_ref[...])
    col = lax.broadcasted_iota(jnp.int32, (1, 3), 1)
    row = jnp.where(col == 0, peaks[0:1, 0:1], jnp.where(col == 1, peaks[1:2, 0:1], peaks[2:3, 0:1]))
    past = hist_ref.shape[0] - 1
    out_ref[0:past, :] = hist_ref[1:, :]
    out_ref[past:, :] = row


def ring_offsets(n):
    offsets = [0]
    for step in range(1, n // 2):
        offsets += [step, -step]
    return offsets + [n // 2]


def ring(piece, axis, n):
    ahead = [(i, (i - 1) % n) for i in range(n)]
    behind = [(i, (i + 1) % n) for i in range(n)]
    pieces, above, below = [piece], piece, piece
    for step in range(1, n // 2):
        above = lax.ppermute(above, axis, ahead)
        below = lax.ppermute(below, axis, behind)
        pieces += [above, below]
    return pieces + [lax.ppermute(above, axis, ahead)]


def per_device(sizes, tokens, w_gate, w_up, upstream, history):
    nh, nx, nw, ny = (sizes[a] for a in "hxwy")
    plane = ("h", "x", "w")
    count = nh * nx * nw
    rows, width = tokens.shape
    depth, units = w_gate.shape
    swap = [(0, 1), (1, 0)]
    spots = [(h, a, b) for h in range(nh) for a in range(nh) for b in range(2)]
    at = lambda h, a, b: h * ny + 2 * (a % nh) + b
    along_y = [(at(h, a, b), at(h, a + h, b)) for h, a, b in spots]
    along_z = [(at(h, a, b), at((a - h) % nh, a, b)) for h, a, b in spots]
    back_y = [(j, i) for i, j in along_y]
    core = lax.axis_index("c")
    place = jnp.stack([core, lax.axis_index("h"), lax.axis_index("y")])

    copies, scal = call(scale_body, [((count, rows, width), BF16), ((8, 128), F32)], (history, tokens))
    x_all = lax.all_to_all(copies, plane, 0, 0, tiled=True)
    gate_other = lax.ppermute(w_gate, "c", swap)
    lift_other = lax.ppermute(w_up, "c", swap)
    up = lax.ppermute(upstream, ("h", "y"), along_y)
    x_all, gate_other, lift_other, up = lax.optimization_barrier((x_all, gate_other, lift_other, up))

    work = 8 * nh * rows * depth * units
    parts, x_mine = call(
        forward_body,
        [((ny, 2 * rows, units), BF16), ((nh * rows, depth), BF16)],
        (place, x_all, w_gate, w_up, gate_other, lift_other),
        flops=work,
        moved=6 * 2**20,
    )
    parts, x_mine, up = lax.optimization_barrier((parts, x_mine, up))
    sums = lax.all_to_all(parts, "y", 0, 0, tiled=True)
    up = lax.ppermute(up, ("h", "y"), along_z)
    x_other = lax.ppermute(x_mine, "c", swap)
    sums, up, x_other = lax.optimization_barrier((sums, up, x_other))
    hidden, quants = call(
        middle_body, [((rows, units), BF16), ((2 * rows + 8, units), BF16)], (sums, up, scal), moved=2**21
    )
    pieces = ring(quants, "y", ny)
    hidden = lax.ppermute(hidden, ("h", "y"), along_z)
    *pieces, hidden = lax.optimization_barrier((*pieces, hidden))
    (back,) = call(
        backward_body,
        [((nx, nh * nw * rows + 8, width), BF16)],
        (place, *pieces, w_gate, w_up, gate_other, lift_other),
        flops=work,
        moved=6 * 2**20,
        scratch=[pltpu.VMEM((2, 2, nh * rows, units), BF16)],
    )
    *pieces, back, hidden = lax.optimization_barrier((*pieces, back, hidden))
    back_cols = lax.all_to_all(back, "x", 0, 0, tiled=True)
    hidden = lax.ppermute(hidden, ("h", "y"), back_y)
    q_mine, q_send = call(
        pick_body,
        [((2, nh * rows, units), BF16)] * 2,
        (place, *pieces),
        moved=2**22,
        scratch=[pltpu.VMEM((2, 2, nh * rows, units), BF16)],
    )
    q_other = lax.ppermute(q_send, "c", swap)
    divisor = scal[0, 0] * scal[1, 0] * (2 * nh * rows)
    contract = (((0,), (0,)), ((), ()))
    grads = []
    for i in range(2):
        total = lax.dot_general(x_mine, q_mine[i], contract, preferred_element_type=F32) + lax.dot_general(
            x_other, q_other[i], contract, preferred_element_type=F32
        )
        grads.append((total / divisor).astype(BF16))
    (column,) = call(column_body, [((nh * nw, rows + 8, width), BF16)], (back_cols,), moved=2**21)
    back_all = lax.all_to_all(column, ("h", "w"), 0, 0, tiled=True)
    back_all, hidden, *grads = lax.optimization_barrier((back_all, hidden, *grads))
    input_grad, peaks, hidden = call(
        last_body,
        [((rows, width), BF16), ((8, 128), F32), ((rows, units), BF16)],
        (back_all, scal, hidden),
        moved=2**21,
    )
    peaks_other = lax.ppermute(peaks, "c", swap)
    (new_history,) = call(history_body, [(history.shape, F32)], (history, peaks, peaks_other))
    return (hidden, input_grad, grads[0], grads[1], new_history)


def solution(mesh):
    sizes = dict(h=mesh.shape["row"] // 2, c=2, x=mesh.shape["col"] // 2, w=2, y=mesh.shape["dep"])
    fine = Mesh(mesh.devices.reshape(tuple(sizes.values())), tuple(sizes))
    row, col = ("h", "c"), ("x", "w")
    placed = (
        P(row, ("y",) + col),
        P("y", col + row),
        P("y", col + row),
        P(row, col + ("y",)),
        P(),
    )

    def step(*args):
        return per_device(sizes, *args)

    return jax.shard_map(
        step,
        mesh=fine,
        in_specs=placed,
        out_specs=(P(row, col + ("y",)), P(row, ("y",) + col), P("y", col + row), P("y", col + row), P()),
        check_vma=False,
    )
```

```python
import functools

import jax
import jax.numpy as jnp
from jax import lax
from jax.experimental import pallas as pl
from jax.experimental.pallas import tpu as pltpu
from jax.sharding import Mesh
from jax.sharding import PartitionSpec as P

F32 = jnp.float32
BF16 = jnp.bfloat16
VMEM = pl.BlockSpec(memory_space=pltpu.VMEM)
SMEM = pl.BlockSpec(memory_space=pltpu.SMEM)


def params():
    return pltpu.CompilerParams(vmem_limit_bytes=16 * 1024 * 1024)


def call(body, outs, args, flops=0, moved=0, scratch=()):
    return pl.pallas_call(
        body,
        out_shape=[jax.ShapeDtypeStruct(s, t) for s, t in outs],
        in_specs=[SMEM if a.dtype == jnp.int32 else VMEM for a in args],
        out_specs=[VMEM] * len(outs),
        scratch_shapes=list(scratch),
        compiler_params=params(),
        cost_estimate=pl.CostEstimate(flops=flops, bytes_accessed=moved, transcendentals=0),
    )(*args)


def top(values):
    return jnp.max(jnp.max(values, axis=0, keepdims=True), axis=1, keepdims=True)


def rows_of(*values):
    row = lax.broadcasted_iota(jnp.int32, (8, 128), 0)
    tile = jnp.zeros((8, 128), F32)
    for i, v in enumerate(values):
        tile = jnp.where(row == i, v, tile)
    return tile


def pack_peaks(peak_in, peak_hidden, peak_grad):
    high = peak_grad.astype(BF16).astype(F32)
    rest = peak_grad - high
    mid = rest.astype(BF16).astype(F32)
    return rows_of(peak_in, peak_hidden, high, mid, rest - mid).astype(BF16)


def unpack_peaks(packed):
    grads = packed[:, 2, :] + packed[:, 3, :] + packed[:, 4, :]
    return top(packed[:, 0, :]), top(packed[:, 1, :]), top(grads)


def scale_body(hist_ref, tok_ref, out_ref, scal_ref):
    tops = jnp.max(hist_ref[...], axis=0, keepdims=True)
    scale_in = 448.0 / tops[:, 0:1]
    scale_grad = 448.0 / tops[:, 2:3]
    tok = tok_ref[...].astype(F32)
    quant = jnp.clip(tok * scale_in, -448.0, 448.0).astype(BF16)
    for i in range(out_ref.shape[0]):
        out_ref[i] = quant
    scal_ref[...] = rows_of(scale_in, scale_grad, top(jnp.abs(tok)))


def forward_body(place_ref, x_ref, g0_ref, u0_ref, g1_ref, u1_ref, out_ref, xh_ref, above_ref, below_ref):
    count = out_ref.shape[0]
    groups, rows = count // 2, x_ref.shape[1]
    cols = x_ref.shape[0] // groups
    core, turned, me = place_ref[0], place_ref[1], place_ref[2]
    for g in range(groups):
        spot = pl.ds(pl.multiple_of(lax.rem(turned + g, groups) * rows, rows), rows)
        for k in range(cols):
            xh_ref[spot, k * 128 : (k + 1) * 128] = x_ref[g * cols + k]
    x = xh_ref[...]
    for which, pair in enumerate(((g0_ref, u0_ref), (g1_ref, u1_ref))):
        place = core if which == 0 else 1 - core
        for half, w_ref in enumerate(pair):
            part = jnp.dot(x, w_ref[...], preferred_element_type=F32).astype(BF16)
            for g in range(groups):
                out_ref[2 * g + place, half * rows : (half + 1) * rows, :] = part[g * rows : (g + 1) * rows]
    above_ref[...] = out_ref[lax.rem(me + count // 2, count)]
    below_ref[...] = out_ref[lax.rem(me + count // 2 - 1, count)]


def add_body(offset, place_ref, in_ref, parts_ref, out_ref):
    count = parts_ref.shape[0]
    own = parts_ref[lax.rem(place_ref[2] + (count + offset), count)]
    out_ref[...] = (in_ref[...].astype(F32) + own.astype(F32)).astype(BF16)


def middle_body(place_ref, above_ref, below_ref, parts_ref, up_ref, scal_ref, hidden_ref, q_ref):
    rows = up_ref.shape[0]
    sums = above_ref[...].astype(F32) + below_ref[...].astype(F32) + parts_ref[place_ref[2]].astype(F32)
    scale_in = scal_ref[0:1, 0:1]
    scale_grad = scal_ref[1:2, 0:1]
    gate_sum = sums[:rows] / scale_in
    lift_sum = sums[rows:] / scale_in
    sigmoid_gate = 1.0 / (1.0 + jnp.exp(-gate_sum))
    activated = gate_sum * sigmoid_gate
    hidden = (activated * lift_sum).astype(BF16)
    hidden_ref[...] = hidden
    grad_in = up_ref[...].astype(F32)
    grad_gate = grad_in * lift_sum * sigmoid_gate * (1.0 + gate_sum * (1.0 - sigmoid_gate))
    grad_lift = grad_in * activated
    quant_gate = jnp.clip(grad_gate * scale_grad, -448.0, 448.0).astype(BF16)
    quant_lift = jnp.clip(grad_lift * scale_grad, -448.0, 448.0).astype(BF16)
    peak_grad = jnp.maximum(top(jnp.abs(grad_gate)), top(jnp.abs(grad_lift)))
    peaks = pack_peaks(scal_ref[2:3, 0:1], top(jnp.abs(hidden.astype(F32))), peak_grad)
    wide = jnp.concatenate([peaks, peaks], axis=1)
    q_ref[:rows, :] = quant_gate
    q_ref[rows : 2 * rows, :] = quant_lift
    q_ref[2 * rows :, :] = wide


def gather(place_ref, piece_refs, kept_ref):
    count = len(piece_refs)
    rows = (piece_refs[0].shape[0] - 8) // 2
    for offset, ref in zip(ring_offsets(count), piece_refs):
        piece = lax.rem(place_ref[2] + (count + offset), count)
        which = lax.rem(piece + place_ref[0], 2)
        spot = pl.ds(pl.multiple_of(lax.div(piece, 2) * rows, rows), rows)
        for half in range(2):
            kept_ref[which, half, spot, :] = ref[half * rows : (half + 1) * rows, :]


def backward_body(place_ref, *refs):
    g0_ref, u0_ref, g1_ref, u1_ref, out_ref, kept_ref = refs[-6:]
    pieces = refs[:-6]
    rows = (pieces[0].shape[0] - 8) // 2
    groups = len(pieces) // 2
    cols = out_ref.shape[0]
    turned = place_ref[1]
    fine = (out_ref.shape[1] - 8) // (groups * rows)
    contract = (((1,), (1,)), ((), ()))
    gather(place_ref, pieces, kept_ref)
    total = None
    for i, w_ref in enumerate((g0_ref, u0_ref, g1_ref, u1_ref)):
        part = lax.dot_general(kept_ref[i // 2, i % 2], w_ref[...], contract, preferred_element_type=F32)
        total = part if total is None else total + part
    found = [unpack_peaks(ref[2 * rows :, 0:128].astype(F32)[None]) for ref in pieces]
    peaks = found[0]
    for other in found[1:]:
        peaks = [jnp.maximum(a, b) for a, b in zip(peaks, other)]
    packed = pack_peaks(*peaks)
    for k in range(cols):
        for g in range(groups):
            first = lax.rem(groups + g - turned, groups) * (fine * rows)
            for j in range(fine):
                lane = (k * fine + j) * 128
                spot = pl.ds(pl.multiple_of(first + j * rows, rows), rows)
                out_ref[k, spot, :] = total[g * rows : (g + 1) * rows, lane : lane + 128].astype(BF16)
        out_ref[k, groups * fine * rows :, :] = packed


def pick_body(place_ref, *refs):
    mine_ref, send_ref, kept_ref = refs[-3:]
    gather(place_ref, refs[:-3], kept_ref)
    mine_ref[...] = kept_ref[0]
    send_ref[...] = kept_ref[1]


def column_body(in_ref, out_ref):
    blocks, rows = out_ref.shape[0], out_ref.shape[1] - 8
    packed = pack_peaks(*unpack_peaks(in_ref[:, blocks * rows :, :].astype(F32)))
    for i in range(blocks):
        part = jnp.sum(in_ref[:, i * rows : (i + 1) * rows, :].astype(F32), axis=0)
        out_ref[i, :rows, :] = part.astype(BF16)
        out_ref[i, rows:, :] = packed


def last_body(in_ref, scal_ref, hidden_ref, out_ref, peaks_ref, hidden_out_ref):
    rows = out_ref.shape[0]
    out_ref[...] = (jnp.sum(in_ref[:, :rows, :].astype(F32), axis=0) / scal_ref[1:2, 0:1]).astype(BF16)
    peaks_ref[...] = rows_of(*unpack_peaks(in_ref[:, rows:, :].astype(F32)))
    hidden_out_ref[...] = hidden_ref[...]


def history_body(hist_ref, mine_ref, other_ref, out_ref):
    peaks = jnp.maximum(mine_ref[...], other_ref[...])
    col = lax.broadcasted_iota(jnp.int32, (1, 3), 1)
    row = jnp.where(col == 0, peaks[0:1, 0:1], jnp.where(col == 1, peaks[1:2, 0:1], peaks[2:3, 0:1]))
    past = hist_ref.shape[0] - 1
    out_ref[0:past, :] = hist_ref[1:, :]
    out_ref[past:, :] = row


def ring_offsets(n):
    offsets = [0]
    for step in range(1, n // 2):
        offsets += [step, -step]
    return offsets + [n // 2]


def ring(piece, axis, n):
    ahead = [(i, (i - 1) % n) for i in range(n)]
    behind = [(i, (i + 1) % n) for i in range(n)]
    pieces, above, below = [piece], piece, piece
    for step in range(1, n // 2):
        above = lax.ppermute(above, axis, ahead)
        below = lax.ppermute(below, axis, behind)
        pieces += [above, below]
    return pieces + [lax.ppermute(above, axis, ahead)]


def ring_sum(place, parts, above, below, axis, n):
    down = [(i, (i - 1) % n) for i in range(n)]
    onward = [(i, (i + 1) % n) for i in range(n)]
    shape = [(above.shape, BF16)]
    half = n // 2
    for step in range(half):
        above = lax.ppermute(above, axis, down)
        if step < half - 1:
            below = lax.ppermute(below, axis, onward)
            (above,) = call(functools.partial(add_body, step + 1 - half), shape, (place, above, parts))
        if step < half - 2:
            (below,) = call(functools.partial(add_body, half - 2 - step), shape, (place, below, parts))
    return above, below


def per_device(sizes, tokens, w_gate, w_up, upstream, history):
    nh, nx, nw, ny = (sizes[a] for a in "hxwy")
    plane = ("h", "x", "w")
    count = nh * nx * nw
    rows, width = tokens.shape
    depth, units = w_gate.shape
    swap = [(0, 1), (1, 0)]
    spots = [(h, a, b) for h in range(nh) for a in range(nh) for b in range(2)]
    at = lambda h, a, b: h * ny + 2 * (a % nh) + b
    along_y = [(at(h, a, b), at(h, a + h, b)) for h, a, b in spots]
    along_z = [(at(h, a, b), at((a - h) % nh, a, b)) for h, a, b in spots]
    back_y = [(j, i) for i, j in along_y]
    core = lax.axis_index("c")
    place = jnp.stack([core, lax.axis_index("h"), lax.axis_index("y")])

    copies, scal = call(scale_body, [((count, rows, width), BF16), ((8, 128), F32)], (history, tokens))
    x_all = lax.all_to_all(copies, plane, 0, 0, tiled=True)
    gate_other = lax.ppermute(w_gate, "c", swap)
    lift_other = lax.ppermute(w_up, "c", swap)
    up = lax.ppermute(upstream, ("h", "y"), along_y)
    up = lax.ppermute(up, ("h", "y"), along_z)
    x_all, gate_other, lift_other, up = lax.optimization_barrier((x_all, gate_other, lift_other, up))

    work = 8 * nh * rows * depth * units
    block = ((2 * rows, units), BF16)
    parts, x_mine, above, below = call(
        forward_body,
        [((ny, 2 * rows, units), BF16), ((nh * rows, depth), BF16), block, block],
        (place, x_all, w_gate, w_up, gate_other, lift_other),
        flops=work,
        moved=6 * 2**20,
    )
    above, below = ring_sum(place, parts, above, below, "y", ny)
    hidden, quants = call(
        middle_body,
        [((rows, units), BF16), ((2 * rows + 8, units), BF16)],
        (place, above, below, parts, up, scal),
        moved=2**21,
    )
    pieces = ring(quants, "y", ny)
    (back,) = call(
        backward_body,
        [((nx, nh * nw * rows + 8, width), BF16)],
        (place, *pieces, w_gate, w_up, gate_other, lift_other),
        flops=work,
        moved=6 * 2**20,
        scratch=[pltpu.VMEM((2, 2, nh * rows, units), BF16)],
    )
    *pieces, back, hidden, x_mine = lax.optimization_barrier((*pieces, back, hidden, x_mine))
    back_cols = lax.all_to_all(back, "x", 0, 0, tiled=True)
    hidden = lax.ppermute(hidden, ("h", "y"), along_z)
    x_other = lax.ppermute(x_mine, "c", swap)
    q_mine, q_send = call(
        pick_body,
        [((2, nh * rows, units), BF16)] * 2,
        (place, *pieces),
        moved=2**22,
        scratch=[pltpu.VMEM((2, 2, nh * rows, units), BF16)],
    )
    q_other = lax.ppermute(q_send, "c", swap)
    back_cols, hidden, x_other, q_other = lax.optimization_barrier((back_cols, hidden, x_other, q_other))
    (column,) = call(column_body, [((nh * nw, rows + 8, width), BF16)], (back_cols,), moved=2**21)
    back_all = lax.all_to_all(column, ("h", "w"), 0, 0, tiled=True)
    divisor = scal[0, 0] * scal[1, 0] * (2 * nh * rows)
    contract = (((0,), (0,)), ((), ()))
    grads = []
    for i in range(2):
        total = lax.dot_general(x_mine, q_mine[i], contract, preferred_element_type=F32) + lax.dot_general(
            x_other, q_other[i], contract, preferred_element_type=F32
        )
        grads.append((total / divisor).astype(BF16))
    hidden = lax.ppermute(hidden, ("h", "y"), back_y)
    back_all, hidden, *grads = lax.optimization_barrier((back_all, hidden, *grads))
    input_grad, peaks, hidden = call(
        last_body,
        [((rows, width), BF16), ((8, 128), F32), ((rows, units), BF16)],
        (back_all, scal, hidden),
        moved=2**21,
    )
    peaks_other = lax.ppermute(peaks, "c", swap)
    (new_history,) = call(history_body, [(history.shape, F32)], (history, peaks, peaks_other))
    return (hidden, input_grad, grads[0], grads[1], new_history)


def solution(mesh):
    sizes = dict(h=mesh.shape["row"] // 2, c=2, x=mesh.shape["col"] // 2, w=2, y=mesh.shape["dep"])
    fine = Mesh(mesh.devices.reshape(tuple(sizes.values())), tuple(sizes))
    row, col = ("h", "c"), ("x", "w")
    placed = (
        P(row, ("y",) + col),
        P("y", col + row),
        P("y", col + row),
        P(row, col + ("y",)),
        P(),
    )

    def step(*args):
        return per_device(sizes, *args)

    return jax.shard_map(
        step,
        mesh=fine,
        in_specs=placed,
        out_specs=(P(row, col + ("y",)), P(row, ("y",) + col), P("y", col + row), P("y", col + row), P()),
        check_vma=False,
    )
```

```python
import jax
import jax.numpy as jnp
from jax import lax
from jax.experimental import pallas as pl
from jax.experimental.pallas import tpu as pltpu
from jax.sharding import Mesh
from jax.sharding import PartitionSpec as P

F32 = jnp.float32
BF16 = jnp.bfloat16
VMEM = pl.BlockSpec(memory_space=pltpu.VMEM)
SMEM = pl.BlockSpec(memory_space=pltpu.SMEM)


def params():
    return pltpu.CompilerParams(vmem_limit_bytes=28 * 1024 * 1024)


def call(body, outs, args, flops=0, moved=0, scratch=()):
    return pl.pallas_call(
        body,
        out_shape=[jax.ShapeDtypeStruct(s, t) for s, t in outs],
        in_specs=[SMEM if a.dtype == jnp.int32 else VMEM for a in args],
        out_specs=[VMEM] * len(outs),
        scratch_shapes=list(scratch),
        compiler_params=params(),
        cost_estimate=pl.CostEstimate(flops=flops, bytes_accessed=moved, transcendentals=0),
    )(*args)


def top(values):
    return jnp.max(jnp.max(values, axis=0, keepdims=True), axis=1, keepdims=True)


def rows_of(*values):
    row = lax.broadcasted_iota(jnp.int32, (8, 128), 0)
    tile = jnp.zeros((8, 128), F32)
    for i, v in enumerate(values):
        tile = jnp.where(row == i, v, tile)
    return tile


def pack_peaks(peak_in, peak_hidden, peak_grad):
    high = peak_grad.astype(BF16).astype(F32)
    rest = peak_grad - high
    mid = rest.astype(BF16).astype(F32)
    return rows_of(peak_in, peak_hidden, high, mid, rest - mid).astype(BF16)


def unpack_peaks(packed):
    grads = packed[:, 2, :] + packed[:, 3, :] + packed[:, 4, :]
    return top(packed[:, 0, :]), top(packed[:, 1, :]), top(grads)


def scale_body(hist_ref, tok_ref, out_ref, scal_ref):
    tops = jnp.max(hist_ref[...], axis=0, keepdims=True)
    scale_in = 448.0 / tops[:, 0:1]
    scale_grad = 448.0 / tops[:, 2:3]
    tok = tok_ref[...].astype(F32)
    quant = jnp.clip(tok * scale_in, -448.0, 448.0).astype(BF16)
    part = out_ref.shape[1]
    for i in range(out_ref.shape[0]):
        out_ref[i] = quant[i % 2 * part : (i % 2 + 1) * part]
    scal_ref[...] = rows_of(scale_in, scale_grad, top(jnp.abs(tok)))


def forward_body(place_ref, x_ref, *refs):
    w_refs, (out_ref, near_ref, far_ref) = refs[:8], refs[8:]
    groups, rows = out_ref.shape[0], x_ref.shape[1]
    cols = x_ref.shape[0] // (2 * groups)
    core, turned, side = place_ref[0], place_ref[1], place_ref[3]
    for g in range(groups):
        spot = pl.ds(pl.multiple_of(lax.rem(turned + g, groups) * rows, rows), rows)
        for k in range(cols):
            lanes = slice(k * 128, (k + 1) * 128)
            near_ref[spot, lanes] = x_ref[2 * (g * cols + k) + side]
            far_ref[spot, lanes] = x_ref[2 * (g * cols + k) + 1 - side]
    near, far = near_ref[...], far_ref[...]
    for i in range(4):
        place = core if i < 2 else 1 - core
        part = jnp.dot(near, w_refs[i][...], preferred_element_type=F32)
        part = (part + jnp.dot(far, w_refs[4 + i][...], preferred_element_type=F32)).astype(BF16)
        spot = pl.ds(pl.multiple_of((2 * place + i % 2) * rows, rows), rows)
        for g in range(groups):
            out_ref[g, spot, :] = part[g * rows : (g + 1) * rows]


def middle_body(place_ref, in_ref, up_ref, up_got_ref, scal_ref, keep_ref, send_ref, q_ref):
    rows = up_ref.shape[0]
    side = place_ref[3]
    scale_in = scal_ref[0:1, 0:1]
    scale_grad = scal_ref[1:2, 0:1]
    sums = jnp.sum(in_ref[...].astype(F32), axis=0)
    peak_hidden = peak_grad = jnp.zeros((1, 1), F32)
    hiddens = []
    for place in range(2):
        base = 2 * place * rows
        gate_sum = sums[base : base + rows] / scale_in
        lift_sum = sums[base + rows : base + 2 * rows] / scale_in
        sigmoid_gate = 1.0 / (1.0 + jnp.exp(-gate_sum))
        activated = gate_sum * sigmoid_gate
        hidden = (activated * lift_sum).astype(BF16)
        hiddens.append(hidden.astype(F32))
        grad_in = jnp.where(side == place, up_ref[...].astype(F32), up_got_ref[...].astype(F32))
        grad_gate = grad_in * lift_sum * sigmoid_gate * (1.0 + gate_sum * (1.0 - sigmoid_gate))
        grad_lift = grad_in * activated
        quant_gate = jnp.clip(grad_gate * scale_grad, -448.0, 448.0).astype(BF16)
        quant_lift = jnp.clip(grad_lift * scale_grad, -448.0, 448.0).astype(BF16)
        peak_grad = jnp.maximum(peak_grad, jnp.maximum(top(jnp.abs(grad_gate)), top(jnp.abs(grad_lift))))
        peak_hidden = jnp.maximum(peak_hidden, top(jnp.abs(hiddens[-1])))
        for i in range(q_ref.shape[0]):
            q_ref[i, base : base + rows, :] = quant_gate
            q_ref[i, base + rows : base + 2 * rows, :] = quant_lift
    keep_ref[...] = jnp.where(side == 0, hiddens[0], hiddens[1]).astype(BF16)
    send_ref[...] = jnp.where(side == 0, hiddens[1], hiddens[0]).astype(BF16)
    peaks = pack_peaks(scal_ref[2:3, 0:1], peak_hidden, peak_grad)
    wide = jnp.concatenate([peaks, peaks], axis=1)
    for i in range(q_ref.shape[0]):
        q_ref[i, 4 * rows :, :] = wide


def pick(place_ref, q_ref, kept_ref):
    rows = (q_ref.shape[1] - 8) // 4
    for i in range(4):
        place = place_ref[0] if i < 2 else 1 - place_ref[0]
        spot = pl.ds(pl.multiple_of((2 * place + i % 2) * rows, rows), rows)
        for g in range(q_ref.shape[0]):
            kept_ref[i, g * rows : (g + 1) * rows, :] = q_ref[g, spot, :]


def backward_body(place_ref, q_ref, *refs):
    w_refs, (out_ref, kept_ref) = refs[:8], refs[8:]
    groups, rows = q_ref.shape[0], (q_ref.shape[1] - 8) // 4
    cols = out_ref.shape[0]
    fine = (out_ref.shape[1] - 8) // (2 * groups * rows)
    turned, side = place_ref[1], place_ref[3]
    contract = (((1,), (1,)), ((), ()))
    pick(place_ref, q_ref, kept_ref)
    packed = pack_peaks(*unpack_peaks(q_ref[:, 4 * rows :, 0:128].astype(F32)))
    for away in range(2):
        total = None
        for i in range(4):
            part = lax.dot_general(kept_ref[i], w_refs[4 * away + i][...], contract, preferred_element_type=F32)
            total = part if total is None else total + part
        target = side if away == 0 else 1 - side
        for k in range(cols):
            for g in range(groups):
                first = lax.rem(groups + g - turned, groups) * fine
                for j in range(fine):
                    lane = (k * fine + j) * 128
                    spot = pl.ds(pl.multiple_of((2 * (first + j) + target) * rows, rows), rows)
                    out_ref[k, spot, :] = total[g * rows : (g + 1) * rows, lane : lane + 128].astype(BF16)
    for k in range(cols):
        out_ref[k, 2 * groups * fine * rows :, :] = packed


def pick_body(place_ref, q_ref, mine_ref, other_ref, kept_ref):
    pick(place_ref, q_ref, kept_ref)
    mine_ref[...] = kept_ref[0:2]
    other_ref[...] = kept_ref[2:4]


def column_body(in_ref, out_ref):
    blocks, rows = out_ref.shape[0], out_ref.shape[1] - 8
    packed = pack_peaks(*unpack_peaks(in_ref[:, blocks * rows :, :].astype(F32)))
    for i in range(blocks):
        part = jnp.sum(in_ref[:, i * rows : (i + 1) * rows, :].astype(F32), axis=0)
        out_ref[i, :rows, :] = part.astype(BF16)
        out_ref[i, rows:, :] = packed


def last_body(in_ref, scal_ref, hidden_ref, out_ref, peaks_ref, hidden_out_ref):
    rows = in_ref.shape[1] - 8
    for side in range(2):
        total = in_ref[side, :rows, :].astype(F32)
        for i in range(1, in_ref.shape[0] // 2):
            total = total + in_ref[2 * i + side, :rows, :].astype(F32)
        out_ref[side * rows : (side + 1) * rows, :] = (total / scal_ref[1:2, 0:1]).astype(BF16)
    peaks_ref[...] = rows_of(*unpack_peaks(in_ref[:, rows:, :].astype(F32)))
    hidden_out_ref[...] = hidden_ref[...]


def history_body(hist_ref, mine_ref, other_ref, out_ref):
    peaks = jnp.maximum(mine_ref[...], other_ref[...])
    col = lax.broadcasted_iota(jnp.int32, (1, 3), 1)
    row = jnp.where(col == 0, peaks[0:1, 0:1], jnp.where(col == 1, peaks[1:2, 0:1], peaks[2:3, 0:1]))
    past = hist_ref.shape[0] - 1
    out_ref[0:past, :] = hist_ref[1:, :]
    out_ref[past:, :] = row


def per_device(sizes, tokens, w_gate, w_up, upstream, history):
    nh, nx, nw, np = (sizes[a] for a in "hxwp")
    plane, last_stage, column_axis = ("h", "x", "w", "t"), ("h", "w", "t"), ("h", "p", "t")
    rows, width = tokens.shape
    rows = rows // 2
    depth, units = w_gate.shape
    swap = [(0, 1), (1, 0)]
    spots = [(h, a, b) for h in range(nh) for a in range(np) for b in range(2)]
    at = lambda h, a, b: (h * np + a % np) * 2 + b
    along_y = [(at(h, a, b), at(h, a + h, b)) for h, a, b in spots]
    along_z = [(at(h, a, b), at((a - h) % nh, a, b)) for h, a, b in spots]
    back_y = [(j, i) for i, j in along_y]
    side = lax.axis_index("t")
    place = jnp.stack([lax.axis_index("c"), lax.axis_index("h"), lax.axis_index("p"), side])

    copies, scal = call(scale_body, [((2 * nh * nx * nw, rows, width), BF16), ((8, 128), F32)], (history, tokens))
    x_all = lax.all_to_all(copies, plane, 0, 0, tiled=True)
    near = [w_gate, w_up]
    far = [lax.ppermute(w, "t", swap) for w in near]
    near += [lax.ppermute(w, "c", swap) for w in near]
    far += [lax.ppermute(w, "c", swap) for w in far]
    up = lax.ppermute(upstream, column_axis, along_y)
    up = lax.ppermute(up, column_axis, along_z).reshape(2, rows, units)
    up_got = lax.ppermute(lax.dynamic_index_in_dim(up, 1 - side, 0, keepdims=False), "t", swap)
    up = lax.dynamic_index_in_dim(up, side, 0, keepdims=False)
    x_all, up, up_got, *weights = lax.optimization_barrier((x_all, up, up_got, *near, *far))

    work = 16 * nh * rows * depth * units * 2
    parts, x_near, x_far = call(
        forward_body,
        [((np, 4 * rows, units), BF16), ((nh * rows, depth), BF16), ((nh * rows, depth), BF16)],
        (place, x_all, *weights),
        flops=work,
        moved=8 * 2**20,
    )
    sums = lax.all_to_all(parts, "p", 0, 0, tiled=True)
    keep, send, quants = call(
        middle_body,
        [((rows, units), BF16), ((rows, units), BF16), ((np, 4 * rows + 8, units), BF16)],
        (place, sums, up, up_got, scal),
        moved=2**20,
    )
    q_all = lax.all_to_all(quants, "p", 0, 0, tiled=True)
    (back,) = call(
        backward_body,
        [((nx, 2 * nh * nw * rows + 8, width), BF16)],
        (place, q_all, *weights),
        flops=work,
        moved=8 * 2**20,
        scratch=[pltpu.VMEM((4, nh * rows, units), BF16)],
    )
    q_all, back, keep, send, x_near, x_far = lax.optimization_barrier((q_all, back, keep, send, x_near, x_far))
    back_cols = lax.all_to_all(back, "x", 0, 0, tiled=True)
    x_side = lax.ppermute(x_far, "t", swap)
    q_mine, q_send = call(
        pick_body,
        [((2, nh * rows, units), BF16)] * 2,
        (place, q_all),
        moved=2**21,
        scratch=[pltpu.VMEM((4, nh * rows, units), BF16)],
    )
    got = lax.ppermute(send, "t", swap)
    hidden = jnp.where(side == 0, jnp.concatenate([keep, got]), jnp.concatenate([got, keep]))
    hidden = lax.ppermute(hidden, column_axis, along_z)
    q_side = lax.ppermute(q_mine, "t", swap)
    q_send_side = lax.ppermute(q_send, "t", swap)
    x_other = lax.ppermute(x_near, "c", swap)
    q_other = lax.ppermute(q_send, "c", swap)
    back_cols, hidden, x_near, x_side, x_other, q_mine, q_side, q_other, q_send_side = lax.optimization_barrier(
        (back_cols, hidden, x_near, x_side, x_other, q_mine, q_side, q_other, q_send_side)
    )
    (column,) = call(column_body, [((2 * nh * nw, rows + 8, width), BF16)], (back_cols,), moved=2**20)
    back_all = lax.all_to_all(column, last_stage, 0, 0, tiled=True)
    hidden = lax.ppermute(hidden, column_axis, back_y)
    xs = [x_near, x_side, x_other, lax.ppermute(x_side, "c", swap)]
    qs = [q_mine, q_side, q_other, lax.ppermute(q_send_side, "c", swap)]
    divisor = scal[0, 0] * scal[1, 0] * (4 * nh * rows)
    contract = (((0,), (0,)), ((), ()))
    grads = []
    for i in range(2):
        total = sum(lax.dot_general(x, q[i], contract, preferred_element_type=F32) for x, q in zip(xs, qs))
        grads.append((total / divisor).astype(BF16))
    back_all, hidden, *grads = lax.optimization_barrier((back_all, hidden, *grads))
    input_grad, peaks, hidden = call(
        last_body,
        [((2 * rows, width), BF16), ((8, 128), F32), ((2 * rows, units), BF16)],
        (back_all, scal, hidden),
        moved=2**20,
    )
    peaks_other = lax.ppermute(peaks, "c", swap)
    (new_history,) = call(history_body, [(history.shape, F32)], (history, peaks, peaks_other))
    return (hidden, input_grad, grads[0], grads[1], new_history)


def solution(mesh):
    sizes = dict(h=mesh.shape["row"] // 2, c=2, x=mesh.shape["col"] // 2, w=2, p=mesh.shape["dep"] // 2, t=2)
    fine = Mesh(mesh.devices.reshape(tuple(sizes.values())), tuple(sizes))
    row, col, dep = ("h", "c"), ("x", "w"), ("p", "t")
    placed = (P(row, dep + col), P(dep, col + row), P(dep, col + row), P(row, col + dep), P())

    def step(*args):
        return per_device(sizes, *args)

    return jax.shard_map(
        step,
        mesh=fine,
        in_specs=placed,
        out_specs=(P(row, col + dep), P(row, dep + col), P(dep, col + row), P(dep, col + row), P()),
        check_vma=False,
    )
```

```python
import jax
import jax.numpy as jnp
from jax import lax
from jax.experimental import pallas as pl
from jax.experimental.pallas import tpu as pltpu
from jax.sharding import Mesh
from jax.sharding import PartitionSpec as P

F32 = jnp.float32
BF16 = jnp.bfloat16
VMEM = pl.BlockSpec(memory_space=pltpu.VMEM)
SMEM = pl.BlockSpec(memory_space=pltpu.SMEM)


def params():
    return pltpu.CompilerParams(vmem_limit_bytes=28 * 1024 * 1024)


def call(body, outs, args, flops=0, moved=0, scratch=()):
    return pl.pallas_call(
        body,
        out_shape=[jax.ShapeDtypeStruct(s, t) for s, t in outs],
        in_specs=[SMEM if a.dtype == jnp.int32 else VMEM for a in args],
        out_specs=[VMEM] * len(outs),
        scratch_shapes=list(scratch),
        compiler_params=params(),
        cost_estimate=pl.CostEstimate(flops=flops, bytes_accessed=moved, transcendentals=0),
    )(*args)


def top(values):
    return jnp.max(jnp.max(values, axis=0, keepdims=True), axis=1, keepdims=True)


def rows_of(*values):
    row = lax.broadcasted_iota(jnp.int32, (8, 128), 0)
    tile = jnp.zeros((8, 128), F32)
    for i, v in enumerate(values):
        tile = jnp.where(row == i, v, tile)
    return tile


def pack_peaks(peak_in, peak_hidden, peak_grad):
    high = peak_grad.astype(BF16).astype(F32)
    rest = peak_grad - high
    mid = rest.astype(BF16).astype(F32)
    return rows_of(peak_in, peak_hidden, high, mid, rest - mid).astype(BF16)


def unpack_peaks(packed):
    grads = packed[:, 2, :] + packed[:, 3, :] + packed[:, 4, :]
    return top(packed[:, 0, :]), top(packed[:, 1, :]), top(grads)


def scale_body(hist_ref, tok_ref, out_ref, scal_ref):
    tops = jnp.max(hist_ref[...], axis=0, keepdims=True)
    scale_in = 448.0 / tops[:, 0:1]
    scale_grad = 448.0 / tops[:, 2:3]
    tok = tok_ref[...].astype(F32)
    quant = jnp.clip(tok * scale_in, -448.0, 448.0).astype(BF16)
    part = out_ref.shape[1]
    for i in range(out_ref.shape[0]):
        out_ref[i] = quant[i % 2 * part : (i % 2 + 1) * part]
    scal_ref[...] = rows_of(scale_in, scale_grad, top(jnp.abs(tok)))


def forward_body(place_ref, x_ref, *refs):
    w_refs, (out_ref, near_ref, far_ref) = refs[:8], refs[8:]
    groups, rows = out_ref.shape[0], x_ref.shape[1]
    cols = x_ref.shape[0] // (2 * groups)
    core, turned, side = place_ref[0], place_ref[1], place_ref[3]
    for g in range(groups):
        spot = pl.ds(pl.multiple_of(lax.rem(turned + g, groups) * rows, rows), rows)
        for k in range(cols):
            lanes = slice(k * 128, (k + 1) * 128)
            near_ref[spot, lanes] = x_ref[2 * (g * cols + k) + side]
            far_ref[spot, lanes] = x_ref[2 * (g * cols + k) + 1 - side]
    near, far = near_ref[...], far_ref[...]
    for i in range(4):
        place = core if i < 2 else 1 - core
        part = jnp.dot(near, w_refs[i][...], preferred_element_type=F32)
        part = (part + jnp.dot(far, w_refs[4 + i][...], preferred_element_type=F32)).astype(BF16)
        spot = pl.ds(pl.multiple_of((2 * place + i % 2) * rows, rows), rows)
        for g in range(groups):
            out_ref[g, spot, :] = part[g * rows : (g + 1) * rows]


def middle_body(place_ref, in_ref, up_ref, up_got_ref, scal_ref, hidden_ref, q_ref):
    rows = up_ref.shape[0]
    side = place_ref[3]
    scale_in = scal_ref[0:1, 0:1]
    scale_grad = scal_ref[1:2, 0:1]
    sums = jnp.sum(in_ref[...].astype(F32), axis=0)
    peak_hidden = peak_grad = jnp.zeros((1, 1), F32)
    hiddens = []
    for place in range(2):
        base = 2 * place * rows
        gate_sum = sums[base : base + rows] / scale_in
        lift_sum = sums[base + rows : base + 2 * rows] / scale_in
        sigmoid_gate = 1.0 / (1.0 + jnp.exp(-gate_sum))
        activated = gate_sum * sigmoid_gate
        hidden = (activated * lift_sum).astype(BF16)
        hiddens.append(hidden.astype(F32))
        grad_in = jnp.where(side == place, up_ref[...].astype(F32), up_got_ref[...].astype(F32))
        grad_gate = grad_in * lift_sum * sigmoid_gate * (1.0 + gate_sum * (1.0 - sigmoid_gate))
        grad_lift = grad_in * activated
        quant_gate = jnp.clip(grad_gate * scale_grad, -448.0, 448.0).astype(BF16)
        quant_lift = jnp.clip(grad_lift * scale_grad, -448.0, 448.0).astype(BF16)
        peak_grad = jnp.maximum(peak_grad, jnp.maximum(top(jnp.abs(grad_gate)), top(jnp.abs(grad_lift))))
        peak_hidden = jnp.maximum(peak_hidden, top(jnp.abs(hiddens[-1])))
        for i in range(q_ref.shape[0]):
            q_ref[i, base : base + rows, :] = quant_gate
            q_ref[i, base + rows : base + 2 * rows, :] = quant_lift
    hidden_ref[0] = jnp.where(side == 0, hiddens[0], hiddens[1]).astype(BF16)
    hidden_ref[1] = jnp.where(side == 0, hiddens[1], hiddens[0]).astype(BF16)
    peaks = pack_peaks(scal_ref[2:3, 0:1], peak_hidden, peak_grad)
    wide = jnp.concatenate([peaks, peaks], axis=1)
    for i in range(q_ref.shape[0]):
        q_ref[i, 4 * rows :, :] = wide


def pick(place_ref, q_ref, kept_ref):
    rows = (q_ref.shape[1] - 8) // 4
    for i in range(4):
        place = place_ref[0] if i < 2 else 1 - place_ref[0]
        spot = pl.ds(pl.multiple_of((2 * place + i % 2) * rows, rows), rows)
        for g in range(q_ref.shape[0]):
            kept_ref[i, g * rows : (g + 1) * rows, :] = q_ref[g, spot, :]


def backward_body(place_ref, q_ref, *refs):
    w_refs, (out_ref, kept_ref) = refs[:8], refs[8:]
    groups, rows = q_ref.shape[0], (q_ref.shape[1] - 8) // 4
    cols = out_ref.shape[0]
    fine = (out_ref.shape[1] - 8) // (2 * groups * rows)
    turned, side = place_ref[1], place_ref[3]
    contract = (((1,), (1,)), ((), ()))
    pick(place_ref, q_ref, kept_ref)
    packed = pack_peaks(*unpack_peaks(q_ref[:, 4 * rows :, 0:128].astype(F32)))
    for away in range(2):
        total = None
        for i in range(4):
            part = lax.dot_general(kept_ref[i], w_refs[4 * away + i][...], contract, preferred_element_type=F32)
            total = part if total is None else total + part
        target = side if away == 0 else 1 - side
        for k in range(cols):
            for g in range(groups):
                first = lax.rem(groups + g - turned, groups) * fine
                for j in range(fine):
                    lane = (k * fine + j) * 128
                    spot = pl.ds(pl.multiple_of((2 * (first + j) + target) * rows, rows), rows)
                    out_ref[k, spot, :] = total[g * rows : (g + 1) * rows, lane : lane + 128].astype(BF16)
    for k in range(cols):
        out_ref[k, 2 * groups * fine * rows :, :] = packed


def pick_body(place_ref, q_ref, kept_ref, other_ref):
    pick(place_ref, q_ref, kept_ref)
    other_ref[...] = kept_ref[2:4]


def weights_body(*refs):
    x_refs, q_refs, scal_ref, out_refs = refs[:4], refs[4:8], refs[8], refs[9:]
    divisor = scal_ref[0:1, 0:1] * scal_ref[1:2, 0:1] * float(4 * x_refs[0].shape[0])
    contract = (((0,), (0,)), ((), ()))
    for i, out_ref in enumerate(out_refs):
        total = None
        for x_ref, q_ref in zip(x_refs, q_refs):
            part = lax.dot_general(x_ref[...], q_ref[i], contract, preferred_element_type=F32)
            total = part if total is None else total + part
        out_ref[...] = (total / divisor).astype(BF16)


def column_body(in_ref, out_ref):
    blocks, rows = out_ref.shape[0], out_ref.shape[1] - 8
    packed = pack_peaks(*unpack_peaks(in_ref[:, blocks * rows :, :].astype(F32)))
    for i in range(blocks):
        part = jnp.sum(in_ref[:, i * rows : (i + 1) * rows, :].astype(F32), axis=0)
        out_ref[i, :rows, :] = part.astype(BF16)
        out_ref[i, rows:, :] = packed


def last_body(place_ref, in_ref, scal_ref, hidden_ref, got_ref, out_ref, peaks_ref, hidden_out_ref):
    rows = in_ref.shape[1] - 8
    for side in range(2):
        total = in_ref[side, :rows, :].astype(F32)
        for i in range(1, in_ref.shape[0] // 2):
            total = total + in_ref[2 * i + side, :rows, :].astype(F32)
        out_ref[side * rows : (side + 1) * rows, :] = (total / scal_ref[1:2, 0:1]).astype(BF16)
    peaks_ref[...] = rows_of(*unpack_peaks(in_ref[:, rows:, :].astype(F32)))
    for away, ref in enumerate((hidden_ref.at[0], got_ref)):
        half = place_ref[3] if away == 0 else 1 - place_ref[3]
        hidden_out_ref[pl.ds(pl.multiple_of(half * rows, rows), rows), :] = ref[...]


def history_body(hist_ref, mine_ref, other_ref, out_ref):
    peaks = jnp.maximum(mine_ref[...], other_ref[...])
    col = lax.broadcasted_iota(jnp.int32, (1, 3), 1)
    row = jnp.where(col == 0, peaks[0:1, 0:1], jnp.where(col == 1, peaks[1:2, 0:1], peaks[2:3, 0:1]))
    past = hist_ref.shape[0] - 1
    out_ref[0:past, :] = hist_ref[1:, :]
    out_ref[past:, :] = row


def per_device(sizes, tokens, w_gate, w_up, upstream, history):
    nh, nx, nw, np = (sizes[a] for a in "hxwp")
    plane, last_stage, column_axis = ("h", "x", "w", "t"), ("h", "w", "t"), ("h", "p", "t")
    rows, width = tokens.shape
    rows = rows // 2
    depth, units = w_gate.shape
    swap = [(0, 1), (1, 0)]
    spots = [(h, a, b) for h in range(nh) for a in range(np) for b in range(2)]
    at = lambda h, a, b: (h * np + a % np) * 2 + b
    along_y = [(at(h, a, b), at(h, a + h, b)) for h, a, b in spots]
    along_z = [(at(h, a, b), at((a - h) % nh, a, b)) for h, a, b in spots]
    back_y = [(j, i) for i, j in along_y]
    side = lax.axis_index("t")
    place = jnp.stack([lax.axis_index("c"), lax.axis_index("h"), lax.axis_index("p"), side])

    copies, scal = call(scale_body, [((2 * nh * nx * nw, rows, width), BF16), ((8, 128), F32)], (history, tokens))
    x_all = lax.all_to_all(copies, plane, 0, 0, tiled=True)
    near = [w_gate, w_up]
    far = [lax.ppermute(w, "t", swap) for w in near]
    up = lax.ppermute(upstream, column_axis, along_y)
    up = lax.ppermute(up, column_axis, along_z).reshape(2, rows, units)
    up_got = lax.ppermute(lax.dynamic_index_in_dim(up, 1 - side, 0, keepdims=False), "t", swap)
    up = lax.dynamic_index_in_dim(up, side, 0, keepdims=False)
    near += [lax.ppermute(w, "c", swap) for w in near]
    up, up_got, *far = lax.optimization_barrier((up, up_got, *far))
    far += [lax.ppermute(w, "c", swap) for w in far]
    x_all, *weights = lax.optimization_barrier((x_all, *near, *far))

    work = 16 * nh * rows * depth * units * 2
    parts, x_near, x_far = call(
        forward_body,
        [((np, 4 * rows, units), BF16), ((nh * rows, depth), BF16), ((nh * rows, depth), BF16)],
        (place, x_all, *weights),
        flops=work,
        moved=8 * 2**20,
    )
    sums = lax.all_to_all(parts, "p", 0, 0, tiled=True)
    hidden, quants = call(
        middle_body,
        [((2, rows, units), BF16), ((np, 4 * rows + 8, units), BF16)],
        (place, sums, up, up_got, scal),
        moved=2**20,
    )
    q_all = lax.all_to_all(quants, "p", 0, 0, tiled=True)
    hidden = lax.ppermute(hidden, column_axis, along_z)
    (back,) = call(
        backward_body,
        [((nx, 2 * nh * nw * rows + 8, width), BF16)],
        (place, q_all, *weights),
        flops=work,
        moved=8 * 2**20,
        scratch=[pltpu.VMEM((4, nh * rows, units), BF16)],
    )
    q_all, back, hidden, x_near, x_far = lax.optimization_barrier((q_all, back, hidden, x_near, x_far))
    back_cols = lax.all_to_all(back, "x", 0, 0, tiled=True)
    q_mine, q_send = call(
        pick_body,
        [((4, nh * rows, units), BF16), ((2, nh * rows, units), BF16)],
        (place, q_all),
        moved=2**20,
    )
    x_side = lax.ppermute(x_far, "t", swap)
    q_side = lax.ppermute(q_mine, "t", swap)
    x_other = lax.ppermute(x_near, "c", swap)
    q_other = lax.ppermute(q_send, "c", swap)
    back_cols, x_other, q_other = lax.optimization_barrier((back_cols, x_other, q_other))
    (column,) = call(column_body, [((2 * nh * nw, rows + 8, width), BF16)], (back_cols,), moved=2**20)
    back_all = lax.all_to_all(column, last_stage, 0, 0, tiled=True)
    hidden = lax.ppermute(hidden, column_axis, back_y)
    hidden_got = lax.ppermute(hidden[1], "t", swap)
    xs = (x_near, x_side, x_other, lax.ppermute(x_side, "c", swap))
    qs = (q_mine, q_side, q_other, lax.ppermute(q_side[2:], "c", swap))
    grads = call(weights_body, [((depth, units), BF16)] * 2, (*xs, *qs, scal), flops=work, moved=2**22)
    back_all, hidden, hidden_got, *grads = lax.optimization_barrier((back_all, hidden, hidden_got, *grads))
    input_grad, peaks, hidden = call(
        last_body,
        [((2 * rows, width), BF16), ((8, 128), F32), ((2 * rows, units), BF16)],
        (place, back_all, scal, hidden, hidden_got),
        moved=2**20,
    )
    peaks_other = lax.ppermute(peaks, "c", swap)
    (new_history,) = call(history_body, [(history.shape, F32)], (history, peaks, peaks_other))
    return (hidden, input_grad, grads[0], grads[1], new_history)


def solution(mesh):
    sizes = dict(h=mesh.shape["row"] // 2, c=2, x=mesh.shape["col"] // 2, w=2, p=mesh.shape["dep"] // 2, t=2)
    fine = Mesh(mesh.devices.reshape(tuple(sizes.values())), tuple(sizes))
    row, col, dep = ("h", "c"), ("x", "w"), ("p", "t")
    placed = (P(row, dep + col), P(dep, col + row), P(dep, col + row), P(row, col + dep), P())

    def step(*args):
        return per_device(sizes, *args)

    return jax.shard_map(
        step,
        mesh=fine,
        in_specs=placed,
        out_specs=(P(row, col + dep), P(row, dep + col), P(dep, col + row), P(dep, col + row), P()),
        check_vma=False,
    )
```

```python
import jax
import jax.numpy as jnp
from jax import lax
from jax.experimental import pallas as pl
from jax.experimental.pallas import tpu as pltpu
from jax.sharding import Mesh
from jax.sharding import PartitionSpec as P

F32 = jnp.float32
BF16 = jnp.bfloat16
VMEM = pl.BlockSpec(memory_space=pltpu.VMEM)
SMEM = pl.BlockSpec(memory_space=pltpu.SMEM)


def params():
    return pltpu.CompilerParams(vmem_limit_bytes=28 * 1024 * 1024)


def call(body, outs, args, flops=0, moved=0, scratch=()):
    return pl.pallas_call(
        body,
        out_shape=[jax.ShapeDtypeStruct(s, t) for s, t in outs],
        in_specs=[SMEM if a.dtype == jnp.int32 else VMEM for a in args],
        out_specs=[VMEM] * len(outs),
        scratch_shapes=list(scratch),
        compiler_params=params(),
        cost_estimate=pl.CostEstimate(flops=flops, bytes_accessed=moved, transcendentals=0),
    )(*args)


def top(values):
    return jnp.max(jnp.max(values, axis=0, keepdims=True), axis=1, keepdims=True)


def rows_of(*values):
    row = lax.broadcasted_iota(jnp.int32, (8, 128), 0)
    tile = jnp.zeros((8, 128), F32)
    for i, v in enumerate(values):
        tile = jnp.where(row == i, v, tile)
    return tile


def pack_peaks(peak_in, peak_hidden, peak_grad):
    high = peak_grad.astype(BF16).astype(F32)
    rest = peak_grad - high
    mid = rest.astype(BF16).astype(F32)
    return rows_of(peak_in, peak_hidden, high, mid, rest - mid).astype(BF16)


def unpack_peaks(packed):
    grads = packed[:, 2, :] + packed[:, 3, :] + packed[:, 4, :]
    return top(packed[:, 0, :]), top(packed[:, 1, :]), top(grads)


def scale_body(hist_ref, tok_ref, out_ref, scal_ref):
    tops = jnp.max(hist_ref[...], axis=0, keepdims=True)
    scale_in = 448.0 / tops[:, 0:1]
    scale_grad = 448.0 / tops[:, 2:3]
    tok = tok_ref[...].astype(F32)
    quant = jnp.clip(tok * scale_in, -448.0, 448.0).astype(BF16)
    part = out_ref.shape[1]
    for i in range(out_ref.shape[0]):
        out_ref[i] = quant[i % 2 * part : (i % 2 + 1) * part]
    scal_ref[...] = rows_of(scale_in, scale_grad, top(jnp.abs(tok)))


def forward_body(place_ref, x_ref, *refs):
    w_refs, (out_ref, near_ref, far_ref) = refs[:8], refs[8:]
    groups, rows = out_ref.shape[0], x_ref.shape[1]
    cols = x_ref.shape[0] // (2 * groups)
    core, turned, side = place_ref[0], place_ref[1], place_ref[3]
    for g in range(groups):
        spot = pl.ds(pl.multiple_of(lax.rem(turned + g, groups) * rows, rows), rows)
        for k in range(cols):
            lanes = slice(k * 128, (k + 1) * 128)
            near_ref[spot, lanes] = x_ref[2 * (g * cols + k) + side]
            far_ref[spot, lanes] = x_ref[2 * (g * cols + k) + 1 - side]
    near, far = near_ref[...], far_ref[...]
    for i in range(4):
        place = core if i < 2 else 1 - core
        part = jnp.dot(near, w_refs[i][...], preferred_element_type=F32)
        part = (part + jnp.dot(far, w_refs[4 + i][...], preferred_element_type=F32)).astype(BF16)
        spot = pl.ds(pl.multiple_of((2 * place + i % 2) * rows, rows), rows)
        for g in range(groups):
            out_ref[g, spot, :] = part[g * rows : (g + 1) * rows]


def middle_body(place_ref, in_ref, up_ref, up_got_ref, scal_ref, hidden_ref, q_ref):
    rows = up_ref.shape[0]
    side = place_ref[3]
    scale_in = scal_ref[0:1, 0:1]
    scale_grad = scal_ref[1:2, 0:1]
    sums = jnp.sum(in_ref[...].astype(F32), axis=0)
    peak_hidden = peak_grad = jnp.zeros((1, 1), F32)
    hiddens = []
    for place in range(2):
        base = 2 * place * rows
        gate_sum = sums[base : base + rows] / scale_in
        lift_sum = sums[base + rows : base + 2 * rows] / scale_in
        sigmoid_gate = 1.0 / (1.0 + jnp.exp(-gate_sum))
        activated = gate_sum * sigmoid_gate
        hidden = (activated * lift_sum).astype(BF16)
        hiddens.append(hidden.astype(F32))
        grad_in = jnp.where(side == place, up_ref[...].astype(F32), up_got_ref[...].astype(F32))
        grad_gate = grad_in * lift_sum * sigmoid_gate * (1.0 + gate_sum * (1.0 - sigmoid_gate))
        grad_lift = grad_in * activated
        quant_gate = jnp.clip(grad_gate * scale_grad, -448.0, 448.0).astype(BF16)
        quant_lift = jnp.clip(grad_lift * scale_grad, -448.0, 448.0).astype(BF16)
        peak_grad = jnp.maximum(peak_grad, jnp.maximum(top(jnp.abs(grad_gate)), top(jnp.abs(grad_lift))))
        peak_hidden = jnp.maximum(peak_hidden, top(jnp.abs(hiddens[-1])))
        for i in range(q_ref.shape[0]):
            q_ref[i, base : base + rows, :] = quant_gate
            q_ref[i, base + rows : base + 2 * rows, :] = quant_lift
    hidden_ref[0] = jnp.where(side == 0, hiddens[0], hiddens[1]).astype(BF16)
    hidden_ref[1] = jnp.where(side == 0, hiddens[1], hiddens[0]).astype(BF16)
    peaks = pack_peaks(scal_ref[2:3, 0:1], peak_hidden, peak_grad)
    wide = jnp.concatenate([peaks, peaks], axis=1)
    for i in range(q_ref.shape[0]):
        q_ref[i, 4 * rows :, :] = wide


def pick(place_ref, q_ref, kept_ref):
    rows = (q_ref.shape[1] - 8) // 4
    for i in range(4):
        place = place_ref[0] if i < 2 else 1 - place_ref[0]
        spot = pl.ds(pl.multiple_of((2 * place + i % 2) * rows, rows), rows)
        for g in range(q_ref.shape[0]):
            kept_ref[i, g * rows : (g + 1) * rows, :] = q_ref[g, spot, :]


def backward_body(place_ref, q_ref, *refs):
    w_refs, (out_ref, kept_ref) = refs[:8], refs[8:]
    groups, rows = q_ref.shape[0], (q_ref.shape[1] - 8) // 4
    cols = out_ref.shape[0]
    fine = (out_ref.shape[1] - 8) // (2 * groups * rows)
    turned, side = place_ref[1], place_ref[3]
    contract = (((1,), (1,)), ((), ()))
    pick(place_ref, q_ref, kept_ref)
    packed = pack_peaks(*unpack_peaks(q_ref[:, 4 * rows :, 0:128].astype(F32)))
    for away in range(2):
        total = None
        for i in range(4):
            part = lax.dot_general(kept_ref[i], w_refs[4 * away + i][...], contract, preferred_element_type=F32)
            total = part if total is None else total + part
        target = side if away == 0 else 1 - side
        for k in range(cols):
            for g in range(groups):
                first = lax.rem(groups + g - turned, groups) * fine
                for j in range(fine):
                    lane = (k * fine + j) * 128
                    spot = pl.ds(pl.multiple_of((2 * (first + j) + target) * rows, rows), rows)
                    out_ref[k, spot, :] = total[g * rows : (g + 1) * rows, lane : lane + 128].astype(BF16)
    for k in range(cols):
        out_ref[k, 2 * groups * fine * rows :, :] = packed


def pick_body(place_ref, q_ref, kept_ref, other_ref):
    pick(place_ref, q_ref, kept_ref)
    other_ref[...] = kept_ref[2:4]


def weights_body(*refs):
    x_refs, q_refs, scal_ref, out_refs = refs[:4], refs[4:8], refs[8], refs[9:]
    divisor = scal_ref[0:1, 0:1] * scal_ref[1:2, 0:1] * float(4 * x_refs[0].shape[0])
    contract = (((0,), (0,)), ((), ()))
    for i, out_ref in enumerate(out_refs):
        total = None
        for x_ref, q_ref in zip(x_refs, q_refs):
            part = lax.dot_general(x_ref[...], q_ref[i], contract, preferred_element_type=F32)
            total = part if total is None else total + part
        out_ref[...] = (total / divisor).astype(BF16)


def column_body(in_ref, out_ref):
    blocks, rows = out_ref.shape[0], out_ref.shape[1] - 8
    packed = pack_peaks(*unpack_peaks(in_ref[:, blocks * rows :, :].astype(F32)))
    for i in range(blocks):
        part = jnp.sum(in_ref[:, i * rows : (i + 1) * rows, :].astype(F32), axis=0)
        out_ref[i, :rows, :] = part.astype(BF16)
        out_ref[i, rows:, :] = packed


def last_body(place_ref, in_ref, scal_ref, hidden_ref, got_ref, out_ref, peaks_ref, hidden_out_ref):
    rows = in_ref.shape[1] - 8
    for side in range(2):
        total = in_ref[side, :rows, :].astype(F32)
        for i in range(1, in_ref.shape[0] // 2):
            total = total + in_ref[2 * i + side, :rows, :].astype(F32)
        out_ref[side * rows : (side + 1) * rows, :] = (total / scal_ref[1:2, 0:1]).astype(BF16)
    peaks_ref[...] = rows_of(*unpack_peaks(in_ref[:, rows:, :].astype(F32)))
    for away, ref in enumerate((hidden_ref.at[0], got_ref)):
        half = place_ref[3] if away == 0 else 1 - place_ref[3]
        hidden_out_ref[pl.ds(pl.multiple_of(half * rows, rows), rows), :] = ref[...]


def history_body(hist_ref, mine_ref, other_ref, out_ref):
    peaks = jnp.maximum(mine_ref[...], other_ref[...])
    col = lax.broadcasted_iota(jnp.int32, (1, 3), 1)
    row = jnp.where(col == 0, peaks[0:1, 0:1], jnp.where(col == 1, peaks[1:2, 0:1], peaks[2:3, 0:1]))
    past = hist_ref.shape[0] - 1
    out_ref[0:past, :] = hist_ref[1:, :]
    out_ref[past:, :] = row


def per_device(sizes, tokens, w_gate, w_up, upstream, history):
    nh, nx, nw, np = (sizes[a] for a in "hxwp")
    plane, last_stage, column_axis = ("h", "x", "w", "t"), ("h", "w", "t"), ("h", "p", "t")
    rows, width = tokens.shape
    rows = rows // 2
    depth, units = w_gate.shape
    swap = [(0, 1), (1, 0)]
    spots = [(h, a, b) for h in range(nh) for a in range(np) for b in range(2)]
    at = lambda h, a, b: (h * np + a % np) * 2 + b
    along_y = [(at(h, a, b), at(h, a + h, b)) for h, a, b in spots]
    along_z = [(at(h, a, b), at((a - h) % nh, a, b)) for h, a, b in spots]
    back_y = [(j, i) for i, j in along_y]
    side = lax.axis_index("t")
    place = jnp.stack([lax.axis_index("c"), lax.axis_index("h"), lax.axis_index("p"), side])

    copies, scal = call(scale_body, [((2 * nh * nx * nw, rows, width), BF16), ((8, 128), F32)], (history, tokens))
    up = lax.ppermute(upstream, column_axis, along_y)
    copies, up = lax.optimization_barrier((copies, up))
    x_all = lax.all_to_all(copies, plane, 0, 0, tiled=True)
    near = [w_gate, w_up]
    far = [lax.ppermute(w, "t", swap) for w in near]
    near += [lax.ppermute(w, "c", swap) for w in near]
    far += [lax.ppermute(w, "c", swap) for w in far]
    x_all, *weights = lax.optimization_barrier((x_all, *near, *far))

    work = 16 * nh * rows * depth * units * 2
    parts, x_near, x_far = call(
        forward_body,
        [((np, 4 * rows, units), BF16), ((nh * rows, depth), BF16), ((nh * rows, depth), BF16)],
        (place, x_all, *weights),
        flops=work,
        moved=8 * 2**20,
    )
    parts, up = lax.optimization_barrier((parts, up))
    sums = lax.all_to_all(parts, "p", 0, 0, tiled=True)
    up = lax.ppermute(up, column_axis, along_z).reshape(2, rows, units)
    up_got = lax.ppermute(lax.dynamic_index_in_dim(up, 1 - side, 0, keepdims=False), "t", swap)
    up = lax.dynamic_index_in_dim(up, side, 0, keepdims=False)
    sums, up, up_got = lax.optimization_barrier((sums, up, up_got))
    hidden, quants = call(
        middle_body,
        [((2, rows, units), BF16), ((np, 4 * rows + 8, units), BF16)],
        (place, sums, up, up_got, scal),
        moved=2**20,
    )
    q_all = lax.all_to_all(quants, "p", 0, 0, tiled=True)
    hidden = lax.ppermute(hidden, column_axis, along_z)
    (back,) = call(
        backward_body,
        [((nx, 2 * nh * nw * rows + 8, width), BF16)],
        (place, q_all, *weights),
        flops=work,
        moved=8 * 2**20,
        scratch=[pltpu.VMEM((4, nh * rows, units), BF16)],
    )
    q_all, back, hidden, x_near, x_far = lax.optimization_barrier((q_all, back, hidden, x_near, x_far))
    back_cols = lax.all_to_all(back, "x", 0, 0, tiled=True)
    q_mine, q_send = call(
        pick_body,
        [((4, nh * rows, units), BF16), ((2, nh * rows, units), BF16)],
        (place, q_all),
        moved=2**20,
    )
    hidden = lax.ppermute(hidden, column_axis, back_y)
    x_far, q_mine, hidden = lax.optimization_barrier((x_far, q_mine, hidden))
    x_side = lax.ppermute(x_far, "t", swap)
    q_side = lax.ppermute(q_mine, "t", swap)
    x_other = lax.ppermute(x_near, "c", swap)
    q_other = lax.ppermute(q_send, "c", swap)
    back_cols, x_other, q_other = lax.optimization_barrier((back_cols, x_other, q_other))
    (column,) = call(column_body, [((2 * nh * nw, rows + 8, width), BF16)], (back_cols,), moved=2**20)
    back_all = lax.all_to_all(column, last_stage, 0, 0, tiled=True)
    hidden_got = lax.ppermute(hidden[1], "t", swap)
    xs = (x_near, x_side, x_other, lax.ppermute(x_side, "c", swap))
    qs = (q_mine, q_side, q_other, lax.ppermute(q_side[2:], "c", swap))
    grads = call(weights_body, [((depth, units), BF16)] * 2, (*xs, *qs, scal))
    back_all, hidden, hidden_got, *grads = lax.optimization_barrier((back_all, hidden, hidden_got, *grads))
    input_grad, peaks, hidden = call(
        last_body,
        [((2 * rows, width), BF16), ((8, 128), F32), ((2 * rows, units), BF16)],
        (place, back_all, scal, hidden, hidden_got),
        moved=2**28,
    )
    peaks_other = lax.ppermute(peaks, "c", swap)
    (new_history,) = call(history_body, [(history.shape, F32)], (history, peaks, peaks_other))
    return (hidden, input_grad, grads[0], grads[1], new_history)


def solution(mesh):
    sizes = dict(h=mesh.shape["row"] // 2, c=2, x=mesh.shape["col"] // 2, w=2, p=mesh.shape["dep"] // 2, t=2)
    fine = Mesh(mesh.devices.reshape(tuple(sizes.values())), tuple(sizes))
    row, col, dep = ("h", "c"), ("x", "w"), ("p", "t")
    placed = (P(row, dep + col), P(dep, col + row), P(dep, col + row), P(row, col + dep), P())

    def step(*args):
        return per_device(sizes, *args)

    return jax.shard_map(
        step,
        mesh=fine,
        in_specs=placed,
        out_specs=(P(row, col + dep), P(row, dep + col), P(dep, col + row), P(dep, col + row), P()),
        check_vma=False,
    )
```

```python
import jax
import jax.numpy as jnp
from jax import lax
from jax.experimental import pallas as pl
from jax.experimental.pallas import tpu as pltpu
from jax.sharding import Mesh
from jax.sharding import PartitionSpec as P

F32 = jnp.float32
BF16 = jnp.bfloat16
STASH = 64
ANY = pl.BlockSpec(memory_space=pl.ANY)
VMEM = pl.BlockSpec(memory_space=pltpu.VMEM)
SMEM = pl.BlockSpec(memory_space=pltpu.SMEM)


def call(body, outs, args, flops=0, moved=0, scratch=(), vmem=48, far=(), far_outs=()):
    return pl.pallas_call(
        body,
        out_shape=[jax.ShapeDtypeStruct(s, t) for s, t in outs],
        in_specs=[SMEM if a.dtype == jnp.int32 else ANY if i in far else VMEM for i, a in enumerate(args)],
        out_specs=[ANY if i in far_outs else VMEM for i in range(len(outs))],
        scratch_shapes=list(scratch),
        compiler_params=pltpu.CompilerParams(vmem_limit_bytes=vmem * 2**20),
        cost_estimate=pl.CostEstimate(flops=flops, bytes_accessed=moved, transcendentals=0),
    )(*args)


def top(values):
    return jnp.max(jnp.max(values, axis=0, keepdims=True), axis=1, keepdims=True)


def rows_of(*values):
    row = lax.broadcasted_iota(jnp.int32, (8, 128), 0)
    tile = jnp.zeros((8, 128), F32)
    for i, v in enumerate(values):
        tile = jnp.where(row == i, v, tile)
    return tile


def pack_peaks(peak_in, peak_hidden, peak_grad):
    high = peak_grad.astype(BF16).astype(F32)
    rest = peak_grad - high
    mid = rest.astype(BF16).astype(F32)
    return rows_of(peak_in, peak_hidden, high, mid, rest - mid).astype(BF16)


def unpack_peaks(packed):
    grads = packed[:, 2, :] + packed[:, 3, :] + packed[:, 4, :]
    return top(packed[:, 0, :]), top(packed[:, 1, :]), top(grads)


def scale_body(hist_ref, tok_ref, out_ref, scal_ref):
    tops = jnp.max(hist_ref[...], axis=0, keepdims=True)
    scale_in = 448.0 / tops[:, 0:1]
    scale_grad = 448.0 / tops[:, 2:3]
    tok = tok_ref[...].astype(F32)
    quant = jnp.clip(tok * scale_in, -448.0, 448.0).astype(BF16)
    for i in range(out_ref.shape[0]):
        out_ref[i] = quant
    scal_ref[...] = rows_of(scale_in, scale_grad, top(jnp.abs(tok)))


def copies_of(source, target, sems):
    return [pltpu.make_async_copy(source(i), target(i), sems.at[i]) for i in range(2)]


def stash_body(g_ref, u_ref, out_ref, sems):
    copies = copies_of(lambda i: (g_ref, u_ref)[i], lambda i: out_ref.at[i], sems)
    for copy in copies:
        copy.start()
    for copy in copies:
        copy.wait()


def forward_body(place_ref, x_ref, g0_ref, u0_ref, stash_ref, out_ref, xh_ref, held_ref, sems):
    copies = copies_of(lambda i: stash_ref.at[i], lambda i: held_ref.at[i], sems)
    for copy in copies:
        copy.start()
    groups, cols, rows = out_ref.shape[0] // 2, x_ref.shape[0] // (out_ref.shape[0] // 2), x_ref.shape[1]
    core, turned = place_ref[0], place_ref[1]
    for g in range(groups):
        spot = pl.ds(pl.multiple_of(lax.rem(turned + g, groups) * rows, rows), rows)
        for k in range(cols):
            xh_ref[spot, k * 128 : (k + 1) * 128] = x_ref[g * cols + k]
    x = xh_ref[...]
    for which, pair in enumerate(((g0_ref, u0_ref), (held_ref.at[0], held_ref.at[1]))):
        place = core if which == 0 else 1 - core
        for half, w_ref in enumerate(pair):
            if which == 1:
                copies[half].wait()
            part = jnp.dot(x, w_ref[...], preferred_element_type=F32).astype(BF16)
            for g in range(groups):
                out_ref[2 * g + place, half * rows : (half + 1) * rows, :] = part[g * rows : (g + 1) * rows]


def middle_body(in_ref, up_ref, scal_ref, hidden_ref, q_ref):
    rows = up_ref.shape[0]
    scale_in = scal_ref[0:1, 0:1]
    scale_grad = scal_ref[1:2, 0:1]
    gate_sum = jnp.sum(in_ref[:, :rows, :].astype(F32), axis=0) / scale_in
    lift_sum = jnp.sum(in_ref[:, rows:, :].astype(F32), axis=0) / scale_in
    sigmoid_gate = 1.0 / (1.0 + jnp.exp(-gate_sum))
    activated = gate_sum * sigmoid_gate
    hidden = (activated * lift_sum).astype(BF16)
    hidden_ref[...] = hidden
    grad_in = up_ref[...].astype(F32)
    grad_gate = grad_in * lift_sum * sigmoid_gate * (1.0 + gate_sum * (1.0 - sigmoid_gate))
    grad_lift = grad_in * activated
    quant_gate = jnp.clip(grad_gate * scale_grad, -448.0, 448.0).astype(BF16)
    quant_lift = jnp.clip(grad_lift * scale_grad, -448.0, 448.0).astype(BF16)
    peak_grad = jnp.maximum(top(jnp.abs(grad_gate)), top(jnp.abs(grad_lift)))
    peaks = pack_peaks(scal_ref[2:3, 0:1], top(jnp.abs(hidden.astype(F32))), peak_grad)
    wide = jnp.concatenate([peaks, peaks], axis=1)
    for i in range(q_ref.shape[0]):
        q_ref[i, :rows, :] = quant_gate
        q_ref[i, rows : 2 * rows, :] = quant_lift
        q_ref[i, 2 * rows :, :] = wide


def backward_body(place_ref, q_ref, g0_ref, u0_ref, stash_ref, out_ref, kept_ref, held_ref, sems):
    copies = copies_of(lambda i: stash_ref.at[i], lambda i: held_ref.at[i], sems)
    for copy in copies:
        copy.start()
    groups = q_ref.shape[0] // 2
    rows = (q_ref.shape[1] - 8) // 2
    cols = out_ref.shape[0] // groups
    core, turned = place_ref[0], place_ref[1]
    contract = (((1,), (1,)), ((), ()))
    total = None
    for which, pair in enumerate(((g0_ref, u0_ref), (held_ref.at[0], held_ref.at[1]))):
        place = core if which == 0 else 1 - core
        for half, w_ref in enumerate(pair):
            if which == 1:
                copies[half].wait()
            for g in range(groups):
                kept_ref[g * rows : (g + 1) * rows, :] = q_ref[2 * g + place, half * rows : (half + 1) * rows, :]
            part = lax.dot_general(kept_ref[...], w_ref[...], contract, preferred_element_type=F32)
            total = part if total is None else total + part
    packed = pack_peaks(*unpack_peaks(q_ref[:, 2 * rows :, 0:128].astype(F32)))
    for g in range(groups):
        first = lax.rem(groups + g - turned, groups) * cols
        for k in range(cols):
            out_ref[first + k, :rows, :] = total[g * rows : (g + 1) * rows, k * 128 : (k + 1) * 128].astype(BF16)
            out_ref[first + k, rows:, :] = packed


def last_body(in_ref, scal_ref, hidden_ref, out_ref, peaks_ref, hidden_out_ref):
    rows = out_ref.shape[0]
    out_ref[...] = (jnp.sum(in_ref[:, :rows, :].astype(F32), axis=0) / scal_ref[1:2, 0:1]).astype(BF16)
    peaks_ref[...] = rows_of(*unpack_peaks(in_ref[:, rows:, :].astype(F32)))
    hidden_out_ref[...] = hidden_ref[...]


def per_device(sizes, tokens, w_gate, w_up, upstream, history):
    nh, nx, nw, ny = (sizes[a] for a in "hxwy")
    plane = ("h", "x", "w")
    count = nh * nx * nw
    rows, width = tokens.shape
    depth, units = w_gate.shape
    swap = [(0, 1), (1, 0)]
    spots = [(h, a, b) for h in range(nh) for a in range(nh) for b in range(2)]
    at = lambda h, a, b: h * ny + 2 * (a % nh) + b
    along_y = [(at(h, a, b), at(h, a + h, b)) for h, a, b in spots]
    along_z = [(at(h, a, b), at((a - h) % nh, a, b)) for h, a, b in spots]
    back_y = [(j, i) for i, j in along_y]
    core = lax.axis_index("c")
    place = jnp.stack([core, lax.axis_index("h")])

    copies, scal = call(scale_body, [((count, rows, width), BF16), ((8, 128), F32)], (history, tokens))
    x_all = lax.all_to_all(copies, plane, 0, 0, tiled=True)
    gate_other = lax.ppermute(w_gate, "c", swap)
    lift_other = lax.ppermute(w_up, "c", swap)
    (stash,) = call(
        stash_body,
        [((STASH, depth, units), BF16)],
        (gate_other, lift_other),
        scratch=[pltpu.SemaphoreType.DMA((2,))],
        far=(0, 1),
        far_outs=(0,),
    )
    held = [pltpu.VMEM((2, depth, units), BF16), pltpu.SemaphoreType.DMA((2,))]
    up = lax.ppermute(upstream, ("h", "y"), along_y)
    x_all, stash, up = lax.optimization_barrier((x_all, stash, up))

    work = 8 * nh * rows * depth * units
    parts, x_mine = call(
        forward_body,
        [((ny, 2 * rows, units), BF16), ((nh * rows, depth), BF16)],
        (place, x_all, w_gate, w_up, stash),
        flops=work,
        moved=6 * 2**20,
        scratch=held,
        vmem=48,
        far=(4,),
    )
    parts, x_mine, up = lax.optimization_barrier((parts, x_mine, up))
    sums = lax.all_to_all(parts, "y", 0, 0, tiled=True)
    up = lax.ppermute(up, ("h", "y"), along_z)
    sums, up = lax.optimization_barrier((sums, up))
    hidden, quants = call(
        middle_body, [((rows, units), BF16), ((ny, 2 * rows + 8, units), BF16)], (sums, up, scal), moved=2**21
    )
    quants, x_mine = lax.optimization_barrier((quants, x_mine))
    q_all = lax.all_to_all(quants, "y", 0, 0, tiled=True)
    hidden = lax.ppermute(hidden, ("h", "y"), along_z)
    x_other = lax.ppermute(x_mine, "c", swap)
    q_all, hidden, x_other = lax.optimization_barrier((q_all, hidden, x_other))
    (back,) = call(
        backward_body,
        [((count, rows + 8, width), BF16)],
        (place, q_all, w_gate, w_up, stash),
        flops=work,
        moved=6 * 2**20,
        scratch=[pltpu.VMEM((nh * rows, units), BF16)] + held,
        vmem=48,
        far=(4,),
    )
    back, q_all, hidden = lax.optimization_barrier((back, q_all, hidden))
    back_all = lax.all_to_all(back, plane, 0, 0, tiled=True)
    hidden = lax.ppermute(hidden, ("h", "y"), back_y)
    q_parts = q_all[:, : 2 * rows].reshape(nh, 2, 2, rows, units)

    def chosen(which):
        part = lax.dynamic_index_in_dim(q_parts, which, 1, keepdims=False)
        return part.transpose(1, 0, 2, 3).reshape(2, nh * rows, units)

    q_other = lax.ppermute(chosen(1 - core), "c", swap)
    q_mine = chosen(core)
    divisor = scal[0, 0] * scal[1, 0] * (2 * nh * rows)
    contract = (((0,), (0,)), ((), ()))
    grads = []
    for i in range(2):
        total = lax.dot_general(x_mine, q_mine[i], contract, preferred_element_type=F32) + lax.dot_general(
            x_other, q_other[i], contract, preferred_element_type=F32
        )
        grads.append((total / divisor).astype(BF16))
    back_all, grads, hidden = lax.optimization_barrier((back_all, grads, hidden))
    input_grad, peaks, hidden = call(
        last_body,
        [((rows, width), BF16), ((8, 128), F32), ((rows, units), BF16)],
        (back_all, scal, hidden),
        moved=2**21,
    )
    peaks_other = lax.ppermute(peaks, "c", swap)
    row = jnp.maximum(peaks, peaks_other)[:3, 0]
    last = lax.broadcasted_iota(jnp.int32, history.shape, 0) == history.shape[0] - 1
    new_history = jnp.where(last, row[None, :], jnp.roll(history, -1, axis=0))
    return (hidden, input_grad, grads[0], grads[1], new_history)


def solution(mesh):
    sizes = dict(h=mesh.shape["row"] // 2, c=2, x=mesh.shape["col"] // 2, w=2, y=mesh.shape["dep"])
    fine = Mesh(mesh.devices.reshape(tuple(sizes.values())), tuple(sizes))
    row, col = ("h", "c"), ("x", "w")
    placed = (
        P(row, ("y",) + col),
        P("y", col + row),
        P("y", col + row),
        P(row, col + ("y",)),
        P(),
    )

    def step(*args):
        return per_device(sizes, *args)

    return jax.shard_map(
        step,
        mesh=fine,
        in_specs=placed,
        out_specs=(P(row, col + ("y",)), P(row, ("y",) + col), P("y", col + row), P("y", col + row), P()),
        check_vma=False,
    )
```

```python
import jax
import jax.numpy as jnp
from jax import lax
from jax.experimental import pallas as pl
from jax.experimental.pallas import tpu as pltpu
from jax.sharding import Mesh
from jax.sharding import PartitionSpec as P

F32 = jnp.float32
BF16 = jnp.bfloat16
STASH = 64
ANY = pl.BlockSpec(memory_space=pl.ANY)
VMEM = pl.BlockSpec(memory_space=pltpu.VMEM)
SMEM = pl.BlockSpec(memory_space=pltpu.SMEM)


def call(body, outs, args, flops=0, moved=0, scratch=(), vmem=48, far=(), far_outs=()):
    return pl.pallas_call(
        body,
        out_shape=[jax.ShapeDtypeStruct(s, t) for s, t in outs],
        in_specs=[SMEM if a.dtype == jnp.int32 else ANY if i in far else VMEM for i, a in enumerate(args)],
        out_specs=[ANY if i in far_outs else VMEM for i in range(len(outs))],
        scratch_shapes=list(scratch),
        compiler_params=pltpu.CompilerParams(vmem_limit_bytes=vmem * 2**20),
        cost_estimate=pl.CostEstimate(flops=flops, bytes_accessed=moved, transcendentals=0),
    )(*args)


def top(values):
    return jnp.max(jnp.max(values, axis=0, keepdims=True), axis=1, keepdims=True)


def rows_of(*values):
    row = lax.broadcasted_iota(jnp.int32, (8, 128), 0)
    tile = jnp.zeros((8, 128), F32)
    for i, v in enumerate(values):
        tile = jnp.where(row == i, v, tile)
    return tile


def pack_peaks(peak_in, peak_hidden, peak_grad):
    high = peak_grad.astype(BF16).astype(F32)
    rest = peak_grad - high
    mid = rest.astype(BF16).astype(F32)
    return rows_of(peak_in, peak_hidden, high, mid, rest - mid).astype(BF16)


def unpack_peaks(packed):
    grads = packed[:, 2, :] + packed[:, 3, :] + packed[:, 4, :]
    return top(packed[:, 0, :]), top(packed[:, 1, :]), top(grads)


def scale_body(hist_ref, tok_ref, out_ref, scal_ref):
    tops = jnp.max(hist_ref[...], axis=0, keepdims=True)
    scale_in = 448.0 / tops[:, 0:1]
    scale_grad = 448.0 / tops[:, 2:3]
    tok = tok_ref[...].astype(F32)
    quant = jnp.clip(tok * scale_in, -448.0, 448.0).astype(BF16)
    for i in range(out_ref.shape[0]):
        out_ref[i] = quant
    scal_ref[...] = rows_of(scale_in, scale_grad, top(jnp.abs(tok)))


def copies_of(source, target, sems):
    cut = source(0).shape[0] // sems.shape[1]
    return [
        pltpu.make_async_copy(
            source(i).at[pl.ds(j * cut, cut)], target(i).at[pl.ds(j * cut, cut)], sems.at[i, j]
        )
        for i in range(2)
        for j in range(sems.shape[1])
    ]


def stash_body(g_ref, u_ref, out_ref, sems):
    copies = copies_of(lambda i: (g_ref, u_ref)[i], lambda i: out_ref.at[i], sems)
    for copy in copies:
        copy.start()
    for copy in copies:
        copy.wait()


def forward_body(place_ref, x_ref, g0_ref, u0_ref, stash_ref, out_ref, xh_ref, held_ref, sems):
    copies = copies_of(lambda i: stash_ref.at[i], lambda i: held_ref.at[i], sems)
    for copy in copies:
        copy.start()
    groups, cols, rows = out_ref.shape[0] // 2, x_ref.shape[0] // (out_ref.shape[0] // 2), x_ref.shape[1]
    core, turned = place_ref[0], place_ref[1]
    for g in range(groups):
        spot = pl.ds(pl.multiple_of(lax.rem(turned + g, groups) * rows, rows), rows)
        for k in range(cols):
            xh_ref[spot, k * 128 : (k + 1) * 128] = x_ref[g * cols + k]
    x = xh_ref[...]
    for which, pair in enumerate(((g0_ref, u0_ref), (held_ref.at[0], held_ref.at[1]))):
        place = core if which == 0 else 1 - core
        for half, w_ref in enumerate(pair):
            if which == 1:
                for copy in copies[half * len(copies) // 2 : (half + 1) * len(copies) // 2]:
                    copy.wait()
            part = jnp.dot(x, w_ref[...], preferred_element_type=F32).astype(BF16)
            for g in range(groups):
                out_ref[2 * g + place, half * rows : (half + 1) * rows, :] = part[g * rows : (g + 1) * rows]


def middle_body(in_ref, up_ref, scal_ref, hidden_ref, q_ref):
    rows = up_ref.shape[0]
    scale_in = scal_ref[0:1, 0:1]
    scale_grad = scal_ref[1:2, 0:1]
    gate_sum = jnp.sum(in_ref[:, :rows, :].astype(F32), axis=0) / scale_in
    lift_sum = jnp.sum(in_ref[:, rows:, :].astype(F32), axis=0) / scale_in
    sigmoid_gate = 1.0 / (1.0 + jnp.exp(-gate_sum))
    activated = gate_sum * sigmoid_gate
    hidden = (activated * lift_sum).astype(BF16)
    hidden_ref[...] = hidden
    grad_in = up_ref[...].astype(F32)
    grad_gate = grad_in * lift_sum * sigmoid_gate * (1.0 + gate_sum * (1.0 - sigmoid_gate))
    grad_lift = grad_in * activated
    quant_gate = jnp.clip(grad_gate * scale_grad, -448.0, 448.0).astype(BF16)
    quant_lift = jnp.clip(grad_lift * scale_grad, -448.0, 448.0).astype(BF16)
    peak_grad = jnp.maximum(top(jnp.abs(grad_gate)), top(jnp.abs(grad_lift)))
    peaks = pack_peaks(scal_ref[2:3, 0:1], top(jnp.abs(hidden.astype(F32))), peak_grad)
    wide = jnp.concatenate([peaks, peaks], axis=1)
    for i in range(q_ref.shape[0]):
        q_ref[i, :rows, :] = quant_gate
        q_ref[i, rows : 2 * rows, :] = quant_lift
        q_ref[i, 2 * rows :, :] = wide


def backward_body(place_ref, q_ref, g0_ref, u0_ref, stash_ref, out_ref, kept_ref, held_ref, sems):
    copies = copies_of(lambda i: stash_ref.at[i], lambda i: held_ref.at[i], sems)
    for copy in copies:
        copy.start()
    groups = q_ref.shape[0] // 2
    rows = (q_ref.shape[1] - 8) // 2
    cols = out_ref.shape[0] // groups
    core, turned = place_ref[0], place_ref[1]
    contract = (((1,), (1,)), ((), ()))
    total = None
    for which, pair in enumerate(((g0_ref, u0_ref), (held_ref.at[0], held_ref.at[1]))):
        place = core if which == 0 else 1 - core
        for half, w_ref in enumerate(pair):
            if which == 1:
                for copy in copies[half * len(copies) // 2 : (half + 1) * len(copies) // 2]:
                    copy.wait()
            for g in range(groups):
                kept_ref[g * rows : (g + 1) * rows, :] = q_ref[2 * g + place, half * rows : (half + 1) * rows, :]
            part = lax.dot_general(kept_ref[...], w_ref[...], contract, preferred_element_type=F32)
            total = part if total is None else total + part
    packed = pack_peaks(*unpack_peaks(q_ref[:, 2 * rows :, 0:128].astype(F32)))
    for g in range(groups):
        first = lax.rem(groups + g - turned, groups) * cols
        for k in range(cols):
            out_ref[first + k, :rows, :] = total[g * rows : (g + 1) * rows, k * 128 : (k + 1) * 128].astype(BF16)
            out_ref[first + k, rows:, :] = packed


def last_body(in_ref, scal_ref, hidden_ref, out_ref, peaks_ref, hidden_out_ref):
    rows = out_ref.shape[0]
    out_ref[...] = (jnp.sum(in_ref[:, :rows, :].astype(F32), axis=0) / scal_ref[1:2, 0:1]).astype(BF16)
    peaks_ref[...] = rows_of(*unpack_peaks(in_ref[:, rows:, :].astype(F32)))
    hidden_out_ref[...] = hidden_ref[...]


def per_device(sizes, tokens, w_gate, w_up, upstream, history):
    nh, nx, nw, ny = (sizes[a] for a in "hxwy")
    plane = ("h", "x", "w")
    count = nh * nx * nw
    rows, width = tokens.shape
    depth, units = w_gate.shape
    swap = [(0, 1), (1, 0)]
    spots = [(h, a, b) for h in range(nh) for a in range(nh) for b in range(2)]
    at = lambda h, a, b: h * ny + 2 * (a % nh) + b
    along_y = [(at(h, a, b), at(h, a + h, b)) for h, a, b in spots]
    along_z = [(at(h, a, b), at((a - h) % nh, a, b)) for h, a, b in spots]
    back_y = [(j, i) for i, j in along_y]
    core = lax.axis_index("c")
    place = jnp.stack([core, lax.axis_index("h")])

    copies, scal = call(scale_body, [((count, rows, width), BF16), ((8, 128), F32)], (history, tokens))
    x_all = lax.all_to_all(copies, plane, 0, 0, tiled=True)
    gate_other = lax.ppermute(w_gate, "c", swap)
    lift_other = lax.ppermute(w_up, "c", swap)
    (stash,) = call(
        stash_body,
        [((STASH, depth, units), BF16)],
        (gate_other, lift_other),
        scratch=[pltpu.SemaphoreType.DMA((2, 4))],
        far=(0, 1),
        far_outs=(0,),
    )
    held = [pltpu.VMEM((2, depth, units), BF16), pltpu.SemaphoreType.DMA((2, 4))]
    up = lax.ppermute(upstream, ("h", "y"), along_y)
    x_all, stash, up = lax.optimization_barrier((x_all, stash, up))

    work = 8 * nh * rows * depth * units
    parts, x_mine = call(
        forward_body,
        [((ny, 2 * rows, units), BF16), ((nh * rows, depth), BF16)],
        (place, x_all, w_gate, w_up, stash),
        flops=work,
        moved=6 * 2**20,
        scratch=held,
        vmem=48,
        far=(4,),
    )
    parts, x_mine, up = lax.optimization_barrier((parts, x_mine, up))
    sums = lax.all_to_all(parts, "y", 0, 0, tiled=True)
    up = lax.ppermute(up, ("h", "y"), along_z)
    sums, up = lax.optimization_barrier((sums, up))
    hidden, quants = call(
        middle_body, [((rows, units), BF16), ((ny, 2 * rows + 8, units), BF16)], (sums, up, scal), moved=2**21
    )
    quants, x_mine = lax.optimization_barrier((quants, x_mine))
    q_all = lax.all_to_all(quants, "y", 0, 0, tiled=True)
    hidden = lax.ppermute(hidden, ("h", "y"), along_z)
    x_other = lax.ppermute(x_mine, "c", swap)
    q_all, hidden, x_other = lax.optimization_barrier((q_all, hidden, x_other))
    (back,) = call(
        backward_body,
        [((count, rows + 8, width), BF16)],
        (place, q_all, w_gate, w_up, stash),
        flops=work,
        moved=6 * 2**20,
        scratch=[pltpu.VMEM((nh * rows, units), BF16)] + held,
        vmem=48,
        far=(4,),
    )
    back, q_all, hidden = lax.optimization_barrier((back, q_all, hidden))
    back_all = lax.all_to_all(back, plane, 0, 0, tiled=True)
    hidden = lax.ppermute(hidden, ("h", "y"), back_y)
    q_parts = q_all[:, : 2 * rows].reshape(nh, 2, 2, rows, units)

    def chosen(which):
        part = lax.dynamic_index_in_dim(q_parts, which, 1, keepdims=False)
        return part.transpose(1, 0, 2, 3).reshape(2, nh * rows, units)

    q_other = lax.ppermute(chosen(1 - core), "c", swap)
    q_mine = chosen(core)
    divisor = scal[0, 0] * scal[1, 0] * (2 * nh * rows)
    contract = (((0,), (0,)), ((), ()))
    grads = []
    for i in range(2):
        total = lax.dot_general(x_mine, q_mine[i], contract, preferred_element_type=F32) + lax.dot_general(
            x_other, q_other[i], contract, preferred_element_type=F32
        )
        grads.append((total / divisor).astype(BF16))
    back_all, grads, hidden = lax.optimization_barrier((back_all, grads, hidden))
    input_grad, peaks, hidden = call(
        last_body,
        [((rows, width), BF16), ((8, 128), F32), ((rows, units), BF16)],
        (back_all, scal, hidden),
        moved=2**21,
    )
    peaks_other = lax.ppermute(peaks, "c", swap)
    row = jnp.maximum(peaks, peaks_other)[:3, 0]
    last = lax.broadcasted_iota(jnp.int32, history.shape, 0) == history.shape[0] - 1
    new_history = jnp.where(last, row[None, :], jnp.roll(history, -1, axis=0))
    return (hidden, input_grad, grads[0], grads[1], new_history)


def solution(mesh):
    sizes = dict(h=mesh.shape["row"] // 2, c=2, x=mesh.shape["col"] // 2, w=2, y=mesh.shape["dep"])
    fine = Mesh(mesh.devices.reshape(tuple(sizes.values())), tuple(sizes))
    row, col = ("h", "c"), ("x", "w")
    placed = (
        P(row, ("y",) + col),
        P("y", col + row),
        P("y", col + row),
        P(row, col + ("y",)),
        P(),
    )

    def step(*args):
        return per_device(sizes, *args)

    return jax.shard_map(
        step,
        mesh=fine,
        in_specs=placed,
        out_specs=(P(row, col + ("y",)), P(row, ("y",) + col), P("y", col + row), P("y", col + row), P()),
        check_vma=False,
    )
```

```python
import jax
import jax.numpy as jnp
from jax import lax
from jax.experimental import pallas as pl
from jax.experimental.pallas import tpu as pltpu
from jax.sharding import Mesh
from jax.sharding import PartitionSpec as P

F32 = jnp.float32
BF16 = jnp.bfloat16
STASH = 64
ANY = pl.BlockSpec(memory_space=pl.ANY)
VMEM = pl.BlockSpec(memory_space=pltpu.VMEM)
SMEM = pl.BlockSpec(memory_space=pltpu.SMEM)


def window(array, block):
    return pl.BlockSpec((1,) + array.shape[1:], lambda i: (block, 0, 0))


def call(body, outs, args, flops=0, moved=0, scratch=(), vmem=48, far=(), far_outs=(), windows=()):
    return pl.pallas_call(
        body,
        grid=(1,) if windows else (),
        out_shape=[jax.ShapeDtypeStruct(s, t) for s, t in outs],
        in_specs=[window(args[i], windows.index(i)) if i in windows else SMEM if a.dtype == jnp.int32 else ANY if i in far else VMEM for i, a in enumerate(args)],
        out_specs=[ANY if i in far_outs else VMEM for i in range(len(outs))],
        scratch_shapes=list(scratch),
        compiler_params=pltpu.CompilerParams(vmem_limit_bytes=vmem * 2**20),
        cost_estimate=pl.CostEstimate(flops=flops, bytes_accessed=moved, transcendentals=0),
    )(*args)


def top(values):
    return jnp.max(jnp.max(values, axis=0, keepdims=True), axis=1, keepdims=True)


def rows_of(*values):
    row = lax.broadcasted_iota(jnp.int32, (8, 128), 0)
    tile = jnp.zeros((8, 128), F32)
    for i, v in enumerate(values):
        tile = jnp.where(row == i, v, tile)
    return tile


def pack_peaks(peak_in, peak_hidden, peak_grad):
    high = peak_grad.astype(BF16).astype(F32)
    rest = peak_grad - high
    mid = rest.astype(BF16).astype(F32)
    return rows_of(peak_in, peak_hidden, high, mid, rest - mid).astype(BF16)


def unpack_peaks(packed):
    grads = packed[:, 2, :] + packed[:, 3, :] + packed[:, 4, :]
    return top(packed[:, 0, :]), top(packed[:, 1, :]), top(grads)


def scale_body(hist_ref, tok_ref, out_ref, scal_ref):
    tops = jnp.max(hist_ref[...], axis=0, keepdims=True)
    scale_in = 448.0 / tops[:, 0:1]
    scale_grad = 448.0 / tops[:, 2:3]
    tok = tok_ref[...].astype(F32)
    quant = jnp.clip(tok * scale_in, -448.0, 448.0).astype(BF16)
    for i in range(out_ref.shape[0]):
        out_ref[i] = quant
    scal_ref[...] = rows_of(scale_in, scale_grad, top(jnp.abs(tok)))


def copies_of(source, target, sems):
    return [pltpu.make_async_copy(source(i), target(i), sems.at[i]) for i in range(2)]


def stash_body(g_ref, u_ref, out_ref, sems):
    copies = copies_of(lambda i: (g_ref, u_ref)[i], lambda i: out_ref.at[i], sems)
    for copy in copies:
        copy.start()
    for copy in copies:
        copy.wait()


def forward_body(place_ref, x_ref, g0_ref, u0_ref, g1_ref, u1_ref, out_ref, xh_ref):
    groups, cols, rows = out_ref.shape[0] // 2, x_ref.shape[0] // (out_ref.shape[0] // 2), x_ref.shape[1]
    core, turned = place_ref[0], place_ref[1]
    for g in range(groups):
        spot = pl.ds(pl.multiple_of(lax.rem(turned + g, groups) * rows, rows), rows)
        for k in range(cols):
            xh_ref[spot, k * 128 : (k + 1) * 128] = x_ref[g * cols + k]
    x = xh_ref[...]
    for which, pair in enumerate(((g0_ref, u0_ref), (g1_ref.at[0], u1_ref.at[0]))):
        place = core if which == 0 else 1 - core
        for half, w_ref in enumerate(pair):
            part = jnp.dot(x, w_ref[...], preferred_element_type=F32).astype(BF16)
            for g in range(groups):
                out_ref[2 * g + place, half * rows : (half + 1) * rows, :] = part[g * rows : (g + 1) * rows]


def middle_body(in_ref, up_ref, scal_ref, hidden_ref, q_ref):
    rows = up_ref.shape[0]
    scale_in = scal_ref[0:1, 0:1]
    scale_grad = scal_ref[1:2, 0:1]
    gate_sum = jnp.sum(in_ref[:, :rows, :].astype(F32), axis=0) / scale_in
    lift_sum = jnp.sum(in_ref[:, rows:, :].astype(F32), axis=0) / scale_in
    sigmoid_gate = 1.0 / (1.0 + jnp.exp(-gate_sum))
    activated = gate_sum * sigmoid_gate
    hidden = (activated * lift_sum).astype(BF16)
    hidden_ref[...] = hidden
    grad_in = up_ref[...].astype(F32)
    grad_gate = grad_in * lift_sum * sigmoid_gate * (1.0 + gate_sum * (1.0 - sigmoid_gate))
    grad_lift = grad_in * activated
    quant_gate = jnp.clip(grad_gate * scale_grad, -448.0, 448.0).astype(BF16)
    quant_lift = jnp.clip(grad_lift * scale_grad, -448.0, 448.0).astype(BF16)
    peak_grad = jnp.maximum(top(jnp.abs(grad_gate)), top(jnp.abs(grad_lift)))
    peaks = pack_peaks(scal_ref[2:3, 0:1], top(jnp.abs(hidden.astype(F32))), peak_grad)
    wide = jnp.concatenate([peaks, peaks], axis=1)
    for i in range(q_ref.shape[0]):
        q_ref[i, :rows, :] = quant_gate
        q_ref[i, rows : 2 * rows, :] = quant_lift
        q_ref[i, 2 * rows :, :] = wide


def backward_body(place_ref, q_ref, g0_ref, u0_ref, g1_ref, u1_ref, out_ref, kept_ref):
    groups = q_ref.shape[0] // 2
    rows = (q_ref.shape[1] - 8) // 2
    cols = out_ref.shape[0] // groups
    core, turned = place_ref[0], place_ref[1]
    contract = (((1,), (1,)), ((), ()))
    total = None
    for which, pair in enumerate(((g0_ref, u0_ref), (g1_ref.at[0], u1_ref.at[0]))):
        place = core if which == 0 else 1 - core
        for half, w_ref in enumerate(pair):
            for g in range(groups):
                kept_ref[g * rows : (g + 1) * rows, :] = q_ref[2 * g + place, half * rows : (half + 1) * rows, :]
            part = lax.dot_general(kept_ref[...], w_ref[...], contract, preferred_element_type=F32)
            total = part if total is None else total + part
    packed = pack_peaks(*unpack_peaks(q_ref[:, 2 * rows :, 0:128].astype(F32)))
    for g in range(groups):
        first = lax.rem(groups + g - turned, groups) * cols
        for k in range(cols):
            out_ref[first + k, :rows, :] = total[g * rows : (g + 1) * rows, k * 128 : (k + 1) * 128].astype(BF16)
            out_ref[first + k, rows:, :] = packed


def last_body(in_ref, scal_ref, hidden_ref, out_ref, peaks_ref, hidden_out_ref):
    rows = out_ref.shape[0]
    out_ref[...] = (jnp.sum(in_ref[:, :rows, :].astype(F32), axis=0) / scal_ref[1:2, 0:1]).astype(BF16)
    peaks_ref[...] = rows_of(*unpack_peaks(in_ref[:, rows:, :].astype(F32)))
    hidden_out_ref[...] = hidden_ref[...]


def per_device(sizes, tokens, w_gate, w_up, upstream, history):
    nh, nx, nw, ny = (sizes[a] for a in "hxwy")
    plane = ("h", "x", "w")
    count = nh * nx * nw
    rows, width = tokens.shape
    depth, units = w_gate.shape
    swap = [(0, 1), (1, 0)]
    spots = [(h, a, b) for h in range(nh) for a in range(nh) for b in range(2)]
    at = lambda h, a, b: h * ny + 2 * (a % nh) + b
    along_y = [(at(h, a, b), at(h, a + h, b)) for h, a, b in spots]
    along_z = [(at(h, a, b), at((a - h) % nh, a, b)) for h, a, b in spots]
    back_y = [(j, i) for i, j in along_y]
    core = lax.axis_index("c")
    place = jnp.stack([core, lax.axis_index("h")])

    copies, scal = call(scale_body, [((count, rows, width), BF16), ((8, 128), F32)], (history, tokens))
    x_all = lax.all_to_all(copies, plane, 0, 0, tiled=True)
    gate_other = lax.ppermute(w_gate, "c", swap)
    lift_other = lax.ppermute(w_up, "c", swap)
    (stash,) = call(
        stash_body,
        [((STASH, depth, units), BF16)],
        (gate_other, lift_other),
        scratch=[pltpu.SemaphoreType.DMA((2,))],
        far=(0, 1),
        far_outs=(0,),
    )
    up = lax.ppermute(upstream, ("h", "y"), along_y)
    x_all, stash, up = lax.optimization_barrier((x_all, stash, up))

    work = 8 * nh * rows * depth * units
    parts, x_mine = call(
        forward_body,
        [((ny, 2 * rows, units), BF16), ((nh * rows, depth), BF16)],
        (place, x_all, w_gate, w_up, stash, stash),
        flops=work,
        moved=6 * 2**20,
        vmem=48,
        windows=(4, 5),
    )
    parts, x_mine, up = lax.optimization_barrier((parts, x_mine, up))
    sums = lax.all_to_all(parts, "y", 0, 0, tiled=True)
    up = lax.ppermute(up, ("h", "y"), along_z)
    sums, up = lax.optimization_barrier((sums, up))
    hidden, quants = call(
        middle_body, [((rows, units), BF16), ((ny, 2 * rows + 8, units), BF16)], (sums, up, scal), moved=2**21
    )
    quants, x_mine = lax.optimization_barrier((quants, x_mine))
    q_all = lax.all_to_all(quants, "y", 0, 0, tiled=True)
    hidden = lax.ppermute(hidden, ("h", "y"), along_z)
    x_other = lax.ppermute(x_mine, "c", swap)
    q_all, hidden, x_other = lax.optimization_barrier((q_all, hidden, x_other))
    (back,) = call(
        backward_body,
        [((count, rows + 8, width), BF16)],
        (place, q_all, w_gate, w_up, stash, stash),
        flops=work,
        moved=6 * 2**20,
        scratch=[pltpu.VMEM((nh * rows, units), BF16)],
        vmem=48,
        windows=(4, 5),
    )
    back, q_all, hidden = lax.optimization_barrier((back, q_all, hidden))
    back_all = lax.all_to_all(back, plane, 0, 0, tiled=True)
    hidden = lax.ppermute(hidden, ("h", "y"), back_y)
    q_parts = q_all[:, : 2 * rows].reshape(nh, 2, 2, rows, units)

    def chosen(which):
        part = lax.dynamic_index_in_dim(q_parts, which, 1, keepdims=False)
        return part.transpose(1, 0, 2, 3).reshape(2, nh * rows, units)

    q_other = lax.ppermute(chosen(1 - core), "c", swap)
    q_mine = chosen(core)
    divisor = scal[0, 0] * scal[1, 0] * (2 * nh * rows)
    contract = (((0,), (0,)), ((), ()))
    grads = []
    for i in range(2):
        total = lax.dot_general(x_mine, q_mine[i], contract, preferred_element_type=F32) + lax.dot_general(
            x_other, q_other[i], contract, preferred_element_type=F32
        )
        grads.append((total / divisor).astype(BF16))
    back_all, grads, hidden = lax.optimization_barrier((back_all, grads, hidden))
    input_grad, peaks, hidden = call(
        last_body,
        [((rows, width), BF16), ((8, 128), F32), ((rows, units), BF16)],
        (back_all, scal, hidden),
        moved=2**21,
    )
    peaks_other = lax.ppermute(peaks, "c", swap)
    row = jnp.maximum(peaks, peaks_other)[:3, 0]
    last = lax.broadcasted_iota(jnp.int32, history.shape, 0) == history.shape[0] - 1
    new_history = jnp.where(last, row[None, :], jnp.roll(history, -1, axis=0))
    return (hidden, input_grad, grads[0], grads[1], new_history)


def solution(mesh):
    sizes = dict(h=mesh.shape["row"] // 2, c=2, x=mesh.shape["col"] // 2, w=2, y=mesh.shape["dep"])
    fine = Mesh(mesh.devices.reshape(tuple(sizes.values())), tuple(sizes))
    row, col = ("h", "c"), ("x", "w")
    placed = (
        P(row, ("y",) + col),
        P("y", col + row),
        P("y", col + row),
        P(row, col + ("y",)),
        P(),
    )

    def step(*args):
        return per_device(sizes, *args)

    return jax.shard_map(
        step,
        mesh=fine,
        in_specs=placed,
        out_specs=(P(row, col + ("y",)), P(row, ("y",) + col), P("y", col + row), P("y", col + row), P()),
        check_vma=False,
    )
```

```python
import jax
import jax.numpy as jnp
from jax import lax
from jax.experimental import pallas as pl
from jax.experimental.pallas import tpu as pltpu
from jax.sharding import Mesh
from jax.sharding import PartitionSpec as P

F32 = jnp.float32
BF16 = jnp.bfloat16
STASH = 64
ANY = pl.BlockSpec(memory_space=pl.ANY)
VMEM = pl.BlockSpec(memory_space=pltpu.VMEM)
SMEM = pl.BlockSpec(memory_space=pltpu.SMEM)


def window(array, block):
    return pl.BlockSpec((1,) + array.shape[1:], lambda i: (block, 0, 0))


def call(body, outs, args, flops=0, moved=0, scratch=(), vmem=48, far=(), far_outs=(), windows=()):
    return pl.pallas_call(
        body,
        grid=(1,) if windows else (),
        out_shape=[jax.ShapeDtypeStruct(s, t) for s, t in outs],
        in_specs=[window(args[i], windows.index(i)) if i in windows else SMEM if a.dtype == jnp.int32 else ANY if i in far else VMEM for i, a in enumerate(args)],
        out_specs=[ANY if i in far_outs else VMEM for i in range(len(outs))],
        scratch_shapes=list(scratch),
        compiler_params=pltpu.CompilerParams(vmem_limit_bytes=vmem * 2**20),
        cost_estimate=pl.CostEstimate(flops=flops, bytes_accessed=moved, transcendentals=0),
    )(*args)


def top(values):
    return jnp.max(jnp.max(values, axis=0, keepdims=True), axis=1, keepdims=True)


def rows_of(*values):
    row = lax.broadcasted_iota(jnp.int32, (8, 128), 0)
    tile = jnp.zeros((8, 128), F32)
    for i, v in enumerate(values):
        tile = jnp.where(row == i, v, tile)
    return tile


def pack_peaks(peak_in, peak_hidden, peak_grad):
    high = peak_grad.astype(BF16).astype(F32)
    rest = peak_grad - high
    mid = rest.astype(BF16).astype(F32)
    return rows_of(peak_in, peak_hidden, high, mid, rest - mid).astype(BF16)


def unpack_peaks(packed):
    grads = packed[:, 2, :] + packed[:, 3, :] + packed[:, 4, :]
    return top(packed[:, 0, :]), top(packed[:, 1, :]), top(grads)


def scale_body(hist_ref, tok_ref, out_ref, scal_ref):
    tops = jnp.max(hist_ref[...], axis=0, keepdims=True)
    scale_in = 448.0 / tops[:, 0:1]
    scale_grad = 448.0 / tops[:, 2:3]
    tok = tok_ref[...].astype(F32)
    quant = jnp.clip(tok * scale_in, -448.0, 448.0).astype(BF16)
    for i in range(out_ref.shape[0]):
        out_ref[i] = quant
    scal_ref[...] = rows_of(scale_in, scale_grad, top(jnp.abs(tok)))


def copies_of(source, target, sems):
    return [pltpu.make_async_copy(source(i), target(i), sems.at[i]) for i in range(2)]


def stash_body(g_ref, u_ref, out_ref, sems):
    copies = copies_of(lambda i: (g_ref, u_ref)[i], lambda i: out_ref.at[i], sems)
    for copy in copies:
        copy.start()
    for copy in copies:
        copy.wait()


def forward_body(place_ref, x_ref, g0_ref, u0_ref, g1_ref, u1_ref, out_ref, xh_ref):
    groups, cols, rows = out_ref.shape[0] // 2, x_ref.shape[0] // (out_ref.shape[0] // 2), x_ref.shape[1]
    core, turned = place_ref[0], place_ref[1]
    for g in range(groups):
        spot = pl.ds(pl.multiple_of(lax.rem(turned + g, groups) * rows, rows), rows)
        for k in range(cols):
            xh_ref[spot, k * 128 : (k + 1) * 128] = x_ref[g * cols + k]
    x = xh_ref[...]
    for which, pair in enumerate(((g0_ref, u0_ref), (g1_ref.at[0], u1_ref.at[0]))):
        place = core if which == 0 else 1 - core
        for half, w_ref in enumerate(pair):
            part = jnp.dot(x, w_ref[...], preferred_element_type=F32).astype(BF16)
            for g in range(groups):
                out_ref[2 * g + place, half * rows : (half + 1) * rows, :] = part[g * rows : (g + 1) * rows]


def middle_body(in_ref, up_ref, scal_ref, hidden_ref, q_ref):
    rows = up_ref.shape[0]
    scale_in = scal_ref[0:1, 0:1]
    scale_grad = scal_ref[1:2, 0:1]
    gate_sum = jnp.sum(in_ref[:, :rows, :].astype(F32), axis=0) / scale_in
    lift_sum = jnp.sum(in_ref[:, rows:, :].astype(F32), axis=0) / scale_in
    sigmoid_gate = 1.0 / (1.0 + jnp.exp(-gate_sum))
    activated = gate_sum * sigmoid_gate
    hidden = (activated * lift_sum).astype(BF16)
    hidden_ref[...] = hidden
    grad_in = up_ref[...].astype(F32)
    grad_gate = grad_in * lift_sum * sigmoid_gate * (1.0 + gate_sum * (1.0 - sigmoid_gate))
    grad_lift = grad_in * activated
    quant_gate = jnp.clip(grad_gate * scale_grad, -448.0, 448.0).astype(BF16)
    quant_lift = jnp.clip(grad_lift * scale_grad, -448.0, 448.0).astype(BF16)
    peak_grad = jnp.maximum(top(jnp.abs(grad_gate)), top(jnp.abs(grad_lift)))
    peaks = pack_peaks(scal_ref[2:3, 0:1], top(jnp.abs(hidden.astype(F32))), peak_grad)
    wide = jnp.concatenate([peaks, peaks], axis=1)
    for i in range(q_ref.shape[0]):
        q_ref[i, :rows, :] = quant_gate
        q_ref[i, rows : 2 * rows, :] = quant_lift
        q_ref[i, 2 * rows :, :] = wide


def backward_body(place_ref, q_ref, g0_ref, u0_ref, g1_ref, u1_ref, out_ref, kept_ref):
    groups = q_ref.shape[0] // 2
    rows = (q_ref.shape[1] - 8) // 2
    cols = out_ref.shape[0] // groups
    core, turned = place_ref[0], place_ref[1]
    contract = (((1,), (1,)), ((), ()))
    total = None
    for which, pair in enumerate(((g0_ref, u0_ref), (g1_ref.at[0], u1_ref.at[0]))):
        place = core if which == 0 else 1 - core
        for half, w_ref in enumerate(pair):
            for g in range(groups):
                kept_ref[g * rows : (g + 1) * rows, :] = q_ref[2 * g + place, half * rows : (half + 1) * rows, :]
            part = lax.dot_general(kept_ref[...], w_ref[...], contract, preferred_element_type=F32)
            total = part if total is None else total + part
    packed = pack_peaks(*unpack_peaks(q_ref[:, 2 * rows :, 0:128].astype(F32)))
    for g in range(groups):
        first = lax.rem(groups + g - turned, groups) * cols
        for k in range(cols):
            out_ref[first + k, :rows, :] = total[g * rows : (g + 1) * rows, k * 128 : (k + 1) * 128].astype(BF16)
            out_ref[first + k, rows:, :] = packed


def peaks_body(in_ref, peaks_ref):
    peaks_ref[...] = rows_of(*unpack_peaks(in_ref[:, in_ref.shape[1] - 8 :, :].astype(F32)))


def last_body(in_ref, scal_ref, hidden_ref, out_ref, hidden_out_ref):
    rows = out_ref.shape[0]
    out_ref[...] = (jnp.sum(in_ref[:, :rows, :].astype(F32), axis=0) / scal_ref[1:2, 0:1]).astype(BF16)
    hidden_out_ref[...] = hidden_ref[...]


def per_device(sizes, tokens, w_gate, w_up, upstream, history):
    nh, nx, nw, ny = (sizes[a] for a in "hxwy")
    plane = ("h", "x", "w")
    count = nh * nx * nw
    rows, width = tokens.shape
    depth, units = w_gate.shape
    swap = [(0, 1), (1, 0)]
    spots = [(h, a, b) for h in range(nh) for a in range(nh) for b in range(2)]
    at = lambda h, a, b: h * ny + 2 * (a % nh) + b
    along_y = [(at(h, a, b), at(h, a + h, b)) for h, a, b in spots]
    along_z = [(at(h, a, b), at((a - h) % nh, a, b)) for h, a, b in spots]
    back_y = [(j, i) for i, j in along_y]
    core = lax.axis_index("c")
    place = jnp.stack([core, lax.axis_index("h")])

    copies, scal = call(scale_body, [((count, rows, width), BF16), ((8, 128), F32)], (history, tokens))
    x_all = lax.all_to_all(copies, plane, 0, 0, tiled=True)
    gate_other = lax.ppermute(w_gate, "c", swap)
    lift_other = lax.ppermute(w_up, "c", swap)
    (stash,) = call(
        stash_body,
        [((STASH, depth, units), BF16)],
        (gate_other, lift_other),
        scratch=[pltpu.SemaphoreType.DMA((2,))],
        far=(0, 1),
        far_outs=(0,),
    )
    up = lax.ppermute(upstream, ("h", "y"), along_y)
    x_all, stash, up = lax.optimization_barrier((x_all, stash, up))

    work = 8 * nh * rows * depth * units
    parts, x_mine = call(
        forward_body,
        [((ny, 2 * rows, units), BF16), ((nh * rows, depth), BF16)],
        (place, x_all, w_gate, w_up, stash, stash),
        flops=work,
        moved=6 * 2**20,
        vmem=48,
        windows=(4, 5),
    )
    parts, x_mine, up = lax.optimization_barrier((parts, x_mine, up))
    sums = lax.all_to_all(parts, "y", 0, 0, tiled=True)
    up = lax.ppermute(up, ("h", "y"), along_z)
    sums, up = lax.optimization_barrier((sums, up))
    hidden, quants = call(
        middle_body, [((rows, units), BF16), ((ny, 2 * rows + 8, units), BF16)], (sums, up, scal), moved=2**21
    )
    quants, x_mine = lax.optimization_barrier((quants, x_mine))
    q_all = lax.all_to_all(quants, "y", 0, 0, tiled=True)
    hidden = lax.ppermute(hidden, ("h", "y"), along_z)
    x_other = lax.ppermute(x_mine, "c", swap)
    q_all, hidden, x_other = lax.optimization_barrier((q_all, hidden, x_other))
    (back,) = call(
        backward_body,
        [((count, rows + 8, width), BF16)],
        (place, q_all, w_gate, w_up, stash, stash),
        flops=work,
        moved=6 * 2**20,
        scratch=[pltpu.VMEM((nh * rows, units), BF16)],
        vmem=48,
        windows=(4, 5),
    )
    back, q_all, hidden = lax.optimization_barrier((back, q_all, hidden))
    back_all = lax.all_to_all(back, plane, 0, 0, tiled=True)
    hidden = lax.ppermute(hidden, ("h", "y"), back_y)
    q_parts = q_all[:, : 2 * rows].reshape(nh, 2, 2, rows, units)

    def chosen(which):
        part = lax.dynamic_index_in_dim(q_parts, which, 1, keepdims=False)
        return part.transpose(1, 0, 2, 3).reshape(2, nh * rows, units)

    q_other = lax.ppermute(chosen(1 - core), "c", swap)
    q_mine = chosen(core)
    divisor = scal[0, 0] * scal[1, 0] * (2 * nh * rows)
    contract = (((0,), (0,)), ((), ()))
    grads = []
    for i in range(2):
        total = lax.dot_general(x_mine, q_mine[i], contract, preferred_element_type=F32) + lax.dot_general(
            x_other, q_other[i], contract, preferred_element_type=F32
        )
        grads.append((total / divisor).astype(BF16))
    back_all, grads, hidden = lax.optimization_barrier((back_all, grads, hidden))
    (peaks,) = call(peaks_body, [((8, 128), F32)], (back_all,))
    input_grad, hidden = call(
        last_body,
        [((rows, width), BF16), ((rows, units), BF16)],
        (back_all, scal, hidden),
        moved=2**21,
    )
    peaks_other = lax.ppermute(peaks, "c", swap)
    row = jnp.maximum(peaks, peaks_other)[:3, 0]
    last = lax.broadcasted_iota(jnp.int32, history.shape, 0) == history.shape[0] - 1
    new_history = jnp.where(last, row[None, :], jnp.roll(history, -1, axis=0))
    return (hidden, input_grad, grads[0], grads[1], new_history)


def solution(mesh):
    sizes = dict(h=mesh.shape["row"] // 2, c=2, x=mesh.shape["col"] // 2, w=2, y=mesh.shape["dep"])
    fine = Mesh(mesh.devices.reshape(tuple(sizes.values())), tuple(sizes))
    row, col = ("h", "c"), ("x", "w")
    placed = (
        P(row, ("y",) + col),
        P("y", col + row),
        P("y", col + row),
        P(row, col + ("y",)),
        P(),
    )

    def step(*args):
        return per_device(sizes, *args)

    return jax.shard_map(
        step,
        mesh=fine,
        in_specs=placed,
        out_specs=(P(row, col + ("y",)), P(row, ("y",) + col), P("y", col + row), P("y", col + row), P()),
        check_vma=False,
    )
```
